512 devices in a mesh: az: 16 (over y, core), ax: 32 (over x, z).
Axes of the slice: x: 4, y: 8, z: 8, core: 2. Of those that a mesh axis runs over, the one named last changes fastest.
Arguments:
- velocity: float32 [3, 512, 256, 256], P(None, 'az', 'ax'), may hold values from -6 to 6
- bubble_slip: float32 [3, 1048576], P(None, ('az', 'ax')), may hold values from -6 to 6
- bubble_size: float32 [1048576], P(('az', 'ax')), may hold values from 0.3 to 3
- bubble_growth: float32 [1048576], P(('az', 'ax')), may hold values from -6 to 6
- bubble_tile: int32 [1048576], P(('az', 'ax')), may hold values from 0 to 511
- bubble_lane: int32 [1048576], P(('az', 'ax')), may hold values from 0 to 127
- send_counts: int32 [512, 32], P(('az', 'ax')), may hold values from 0 to 128, as said below
- bubble_order: int32 [512, 2048], P(('az', 'ax')), may hold values from 0 to 2047, each once within a row
- radial_inverse: bfloat16 [256, 256, 256], P('az'), may hold values from -0.375 to 0.375
Outputs:
- predicted: float32 [3, 512, 256, 256], P(None, 'az', 'ax')
- pressure_modes: float32 [512, 256, 256], P('az', 'ax')
The draws below stay inside these ranges and needn't reach their ends.
Inputs may be any that keep to these rules, and one draw needn't show every extreme that they name: `send_counts`: each row sums to 2048. In each azimuthal group one owner index, the same for all holders of the group and drawn from the seed, gets 128 from every holder; each row's other counts are one zero and pairs that sum to 128. `bubble_order`: row h is a permutation of 0 to 2047 listing holder h's bubbles by owner: the first send_counts[h, 0] go to ax index 0, the next send_counts[h, 1] to ax index 1, and so on.
All inputs are finite; a program needn't handle non-finite values.
Results may differ from the reference program's by a relative error of at most 0.009.
Values may be sent and summed in bfloat16 or wider, within the bound.
No kernel may reach another device: no remote copies, remote signals or barrier semaphores. Data moves between devices by JAX's collectives and lax.ppermute only.
A program may use at most 64 MiB of HBM per device.

```python
import math
import jax
import jax.numpy as jnp
from jax import lax

NTH = 512
NR = 256
AX_DEV = 8
BUB_DEV = 2048
TH_DEV = 32
NX = 256
CAP = 128
NBUB = 1048576
TILES = 512
PAIRS = 256
N_AZ = 16
N_AX = 32
DEVICES = 512


def draw_send_counts(key, part):
    key_chosen, key_scores, key_shares = jax.random.split(jax.random.fold_in(key, 11), 3)
    holders = N_AZ * N_AX
    chosen = jax.random.randint(key_chosen, (N_AZ,), 0, N_AX)
    chosen_row = jnp.repeat(chosen, N_AX)
    column = jnp.arange(N_AX, dtype=jnp.int32)
    scores = jax.random.randint(key_scores, (holders, N_AX), 0, 1 << 20) * N_AX + column[None, :]
    scores = jnp.where(column[None, :] == chosen_row[:, None], jnp.int32(1 << 30), scores)
    ranking = jnp.argsort(scores, axis=1)
    half_count = (N_AX - 2) // 2
    split_share = jax.random.randint(key_shares, (holders, half_count), 0, CAP + 1)
    values = jnp.concatenate([split_share, CAP - split_share, jnp.zeros((holders, 1), jnp.int32), jnp.full((holders, 1), CAP, jnp.int32)], axis=1)
    holder_rows = jnp.arange(holders, dtype=jnp.int32)[:, None]
    return jnp.zeros((holders, N_AX), jnp.int32).at[holder_rows, ranking].set(values)


def plant(array, stream_key, smallest, high):
    spot = [jax.random.randint(jax.random.fold_in(stream_key, axis), (), 0, length) for axis, length in enumerate(array.shape)]
    longest = array.shape.index(max(array.shape))
    neighbour = spot[:longest] + [(spot[longest] + 1) % array.shape[longest]] + spot[longest + 1:]
    return array.at[tuple(spot)].set(smallest).at[tuple(neighbour)].set(high)


def shard_levels(rng, extent, cuts, low, top_value):
    factor_of = 1.0
    for dim, parts in cuts:
        steps = jax.random.uniform(jax.random.fold_in(jax.random.fold_in(rng, 6), dim), (parts,), jnp.float32, low / len(cuts), top_value / len(cuts))
        factor_of = factor_of * jnp.repeat(jnp.exp(steps), extent[dim] // parts).reshape((-1,) + (1,) * (len(extent) - 1 - dim))
    return factor_of


def centred(rng, dims, deviation, reach, cuts=(), kind=jnp.bfloat16):
    result = deviation * jax.random.normal(rng, dims, jnp.float32)
    if cuts:
        result = result * shard_levels(rng, dims, cuts, -0.22, 0.18)
    return jnp.clip(result, -reach, reach).astype(kind)


def setup_inputs(seed: int = 0) -> dict:
    streams_of = jax.random.split(jax.random.key(seed), 10)
    velocity = centred(streams_of[0], (3, NTH, NX, NR), 1.0, 6.0, ((1, 16), (2, 32)), jnp.float32)
    bubble_slip = centred(streams_of[1], (3, NBUB), 1.0, 6.0, ((1, 512),), jnp.float32)
    bubble_size = jnp.clip(jnp.exp(math.log(3.0) - 2.3025851 * jax.random.uniform(streams_of[2], (NBUB,), jnp.float32) ** shard_levels(streams_of[2], (NBUB,), ((0, 512),), -0.2, 0.2)), 0.3, 3.0)
    bubble_growth = centred(streams_of[3], (NBUB,), 1.0, 6.0, ((0, 512),), jnp.float32)
    bubble_tile = plant(jax.random.randint(streams_of[4], (NBUB,), 0, TILES), jax.random.fold_in(streams_of[4], 1), 0, TILES - 1).astype(jnp.int32)
    bubble_lane = plant(jax.random.randint(streams_of[5], (NBUB,), 0, 128), jax.random.fold_in(streams_of[5], 1), 0, 127).astype(jnp.int32)
    send_counts = draw_send_counts(jax.random.fold_in(streams_of[9], 71), 0)
    bubble_order = jax.vmap(lambda own: jax.random.permutation(own, BUB_DEV))(jax.random.split(streams_of[7], DEVICES)).reshape((DEVICES, BUB_DEV)).astype(jnp.int32)
    radial_inverse = centred(streams_of[8], (PAIRS, NR, NR), NR ** -0.5, 0.375, ((0, 16),))
    return dict(velocity=velocity, bubble_slip=bubble_slip, bubble_size=bubble_size, bubble_growth=bubble_growth, bubble_tile=bubble_tile, bubble_lane=bubble_lane, send_counts=send_counts, bubble_order=bubble_order, radial_inverse=radial_inverse)


DIFFUSE = 0.12

def radial_parts(values):
    zero_rim = jnp.zeros_like(values[..., :1])
    outer = jnp.concatenate([values[..., 1:], zero_rim], axis=-1)
    inner = jnp.concatenate([zero_rim, values[..., :-1]], axis=-1)
    return (outer, inner)

def reference(velocity, bubble_slip, bubble_size, bubble_growth, bubble_tile, bubble_lane, send_counts, bubble_order, radial_inverse):
    strength = jnp.sqrt(1.0 + bubble_slip[0] * bubble_slip[0] + bubble_slip[1] * bubble_slip[1] + bubble_slip[2] * bubble_slip[2])
    bubble_loads = jnp.concatenate([bubble_size * strength * bubble_slip, (bubble_size * bubble_growth)[None]], axis=0)
    holders = send_counts.shape[0]
    slot_ends = jnp.cumsum(send_counts, axis=1)
    position = jnp.arange(BUB_DEV, dtype=jnp.int32)
    destination = lax.optimization_barrier(jnp.sum((position[None, :, None] >= slot_ends[:, None, :]).astype(jnp.int32), axis=2))
    holder_index = jnp.arange(holders, dtype=jnp.int32)[:, None]
    bubble_index = (holder_index * BUB_DEV + bubble_order).reshape(-1)
    destination = destination.reshape(-1)
    group_index = jnp.broadcast_to(holder_index // N_AX, bubble_order.shape).reshape(-1)
    local_cell = bubble_tile[bubble_index] * 128 + bubble_lane[bubble_index]
    theta_index = group_index * TH_DEV + local_cell // (AX_DEV * NR)
    axial_index = destination * AX_DEV + local_cell // NR % AX_DEV
    radial_index = local_cell % NR
    target = (theta_index * NX + axial_index) * NR + radial_index
    density = jnp.zeros((4, NTH * NX * NR), jnp.float32).at[:, target].add(bubble_loads[:, bubble_index])
    density = density.reshape(4, NTH, NX, NR)
    outer, inner = radial_parts(velocity)
    radius = jnp.arange(NR, dtype=jnp.float32)
    axial_term = jnp.roll(velocity, -1, 2) + jnp.roll(velocity, 1, 2) - 2.0 * velocity
    azimuth_term = jnp.roll(velocity, -1, 1) + jnp.roll(velocity, 1, 1) - 2.0 * velocity
    radial_term = ((radius + 1.0) * (outer - velocity) - radius * (velocity - inner)) / (radius + 0.5)
    predicted = velocity + DIFFUSE * (axial_term + azimuth_term + radial_term) + density[:3]
    divergence = 0.5 * (jnp.roll(velocity[0], -1, 1) - jnp.roll(velocity[0], 1, 1))
    divergence = divergence + 0.5 * (jnp.roll(velocity[1], -1, 0) - jnp.roll(velocity[1], 1, 0))
    divergence = divergence + ((radius + 1.0) * outer[2] - radius * inner[2]) / (2.0 * radius + 1.0)
    source = divergence + density[3]
    spectrum = jnp.fft.rfft(source, axis=0)
    half_length = NTH // 2
    cosine_part = spectrum.real[:half_length]
    sine_part = (-spectrum.imag[:half_length]).at[0].set(spectrum.real[half_length])
    coefficients = jnp.stack([cosine_part, sine_part], axis=1).reshape(NTH, NX, NR) * math.sqrt(2.0 / NTH)
    coefficients = coefficients.astype(jnp.bfloat16)
    grouped = coefficients.reshape(half_length, 2 * NX, NR).astype(jnp.float32)
    pressure_modes = jnp.einsum('jsr,jnr->jns', radial_inverse.astype(jnp.float32), grouped).reshape(NTH, NX, NR)
    return (predicted, pressure_modes)
```

```python
import functools
import math

import jax
import jax.numpy as jnp
import numpy as np
from jax import lax
from jax.experimental import pallas as pl
from jax.experimental.pallas import tpu as pltpu
from jax.sharding import PartitionSpec as P

DIFFUSE = 0.12
LANES = 128
ROWS = 8

VMEM = pl.BlockSpec(memory_space=pltpu.VMEM)
ANY = pl.BlockSpec(memory_space=pl.ANY)


def call(body, name, out_shape, operands, scratch=(), specs=None, flops=0, limit=24):
    moved = sum(x.size * x.dtype.itemsize for x in operands)
    return pl.pallas_call(
        body,
        name=name,
        out_shape=out_shape,
        in_specs=[VMEM] * len(operands) if specs is None else specs,
        out_specs=jax.tree.map(lambda _: VMEM, out_shape),
        scratch_shapes=list(scratch),
        compiler_params=pltpu.CompilerParams(vmem_limit_bytes=limit * 1024 * 1024),
        cost_estimate=pl.CostEstimate(flops=flops, bytes_accessed=moved, transcendentals=0),
    )(*operands)


def take_rows(table, row, lane, shape):
    found = jnp.zeros(shape, table.dtype)
    for r in range(table.shape[0]):
        line = jnp.broadcast_to(table[r : r + 1, :], shape)
        picked = jnp.take_along_axis(line, lane, axis=1, mode="promise_in_bounds")
        found = jnp.where(row == r, picked, found)
    return found


def pack_body(
    slip, size, growth, tile, lane, counts, order, out, listed, slips, payload, staged
):
    lines = listed.shape[0]
    peers = counts.shape[1]
    for j in range(lines):
        span = slice(j * LANES, (j + 1) * LANES)
        listed[j : j + 1, :] = order[0:1, span]
        for k in range(3):
            slips[k, j : j + 1, :] = slip[k : k + 1, span]
    s0, s1, s2 = slips[0], slips[1], slips[2]
    scale = size[...] * jnp.sqrt(1.0 + s0 * s0 + s1 * s1 + s2 * s2)
    payload[0] = scale * s0
    payload[1] = scale * s1
    payload[2] = scale * s2
    payload[3] = size[...] * growth[...]
    payload[4] = (tile[...] * LANES + lane[...]).astype(jnp.float32)
    count_rows = jnp.broadcast_to(counts[...], (peers, peers))
    below = lax.broadcasted_iota(jnp.int32, (peers, peers), 1) < lax.broadcasted_iota(
        jnp.int32, (peers, peers), 0
    )
    own = lax.broadcasted_iota(jnp.int32, (peers, peers), 1) == lax.broadcasted_iota(
        jnp.int32, (peers, peers), 0
    )
    start = jnp.sum(jnp.where(below, count_rows, 0), axis=1, keepdims=True)
    count = jnp.sum(jnp.where(own, count_rows, 0), axis=1, keepdims=True)
    shape = (peers, LANES)
    slot = lax.broadcasted_iota(jnp.int32, shape, 1)
    used = slot < count
    place = jnp.minimum(start + slot, lines * LANES - 1)
    bubble = take_rows(listed, place >> 7, place & 127, shape)
    row, column = bubble >> 7, bubble & 127
    for k in range(4):
        value = take_rows(payload.at[k], row, column, shape)
        staged[:, k, :] = jnp.where(used, value, 0.0)
    cell = take_rows(payload.at[4], row, column, shape).astype(jnp.int32)
    cell = jnp.where(used, cell, 0)
    staged[:, 4, :] = (cell >> 8).astype(jnp.float32)
    staged[:, 5, :] = (cell & 255).astype(jnp.float32)
    staged[:, 6, :] = jnp.zeros(shape, jnp.float32)
    staged[:, 7, :] = jnp.zeros(shape, jnp.float32)
    out[...] = staged[...].astype(jnp.bfloat16)


def edges_body(velocity, _, first_theta, last_theta, first_x, last_x):
    th = velocity.shape[1]
    first_theta[...] = velocity[:, 0].astype(jnp.bfloat16)
    last_theta[...] = velocity[:, th - 1].astype(jnp.bfloat16)
    first_x[...] = velocity[:, :, 0, :].astype(jnp.bfloat16)
    last_x[...] = velocity[:, :, ROWS - 1, :].astype(jnp.bfloat16)


def radial_neighbours(v):
    column = lax.broadcasted_iota(jnp.int32, v.shape, 1)
    last = v.shape[1] - 1
    outer = jnp.where(column == last, 0.0, pltpu.roll(v, last, 1))
    inner = jnp.where(column == 0, 0.0, pltpu.roll(v, 1, 1))
    return outer, inner


def axial_neighbours(v, before, after):
    row = lax.broadcasted_iota(jnp.int32, v.shape, 0)
    ahead = jnp.where(row == ROWS - 1, after, pltpu.roll(v, ROWS - 1, 0))
    behind = jnp.where(row == 0, before, pltpu.roll(v, 1, 0))
    return ahead, behind


def divergence_body(velocity, theta_before, theta_after, x_before, x_after, out, low, high):
    th, width = velocity.shape[1], velocity.shape[3]
    low[...] = x_before[0].astype(jnp.float32)
    high[...] = x_after[0].astype(jnp.float32)
    radius = lax.broadcasted_iota(jnp.int32, (ROWS, width), 1).astype(jnp.float32)
    outward = (radius + 1.0) / (2.0 * radius + 1.0)
    inward = radius / (2.0 * radius + 1.0)
    for t in range(th):
        ahead, behind = axial_neighbours(velocity[0, t], low[t : t + 1, :], high[t : t + 1, :])
        above = velocity[1, t + 1] if t < th - 1 else theta_after[1].astype(jnp.float32)
        under = velocity[1, t - 1] if t > 0 else theta_before[1].astype(jnp.float32)
        outer, inner = radial_neighbours(velocity[2, t])
        out[t] = 0.5 * ((ahead - behind) + (above - under)) + (outward * outer - inward * inner)


def cell_hot(index_line, cells):
    row = lax.broadcasted_iota(jnp.int32, (cells, LANES), 0).astype(jnp.bfloat16)
    return row == jnp.broadcast_to(index_line, (cells, LANES))


def hot_parts(arrived, first, count, across, along):
    cells = across.shape[0]
    zero = jnp.zeros((cells, LANES), jnp.bfloat16)
    for h in range(arrived.shape[0]):
        span = slice(h * LANES, (h + 1) * LANES)
        block = arrived[h]
        across[:, span] = jnp.where(
            cell_hot(block[4:5, :], cells), jnp.ones_like(zero), zero
        )
        here = cell_hot(block[5:6, :], cells)
        for k in range(count):
            value = jnp.broadcast_to(block[first + k : first + k + 1, :], zero.shape)
            along[k, :, span] = jnp.where(here, value, zero)


def deposit(across, along):
    return lax.dot_general(
        across, along, (((1,), (1,)), ((), ())), preferred_element_type=jnp.float32
    )


def source_body(arrived, divergence, out, across, along, whole):
    th = divergence.shape[0]
    hot_parts(arrived, 3, 1, across, along)
    density = deposit(across[...], along[0])
    total = density + divergence[...].reshape(density.shape)
    halves = whole.shape[0]
    for half in range(halves):
        whole[half] = total[:, half * LANES : (half + 1) * LANES]
        for x in range(ROWS):
            layer = whole[half, pl.ds(x, th, stride=ROWS), :]
            out[x * halves + half] = layer.astype(jnp.bfloat16)


def predictor_body(
    arrived, velocity, theta_before, theta_after, x_before, x_after, out, across, along, low, high,
    density,
):
    th, width = velocity.shape[1], velocity.shape[3]
    hot_parts(arrived, 0, 3, across, along)
    radius = lax.broadcasted_iota(jnp.int32, (ROWS, width), 1).astype(jnp.float32)
    outward = (radius + 1.0) / (radius + 0.5)
    inward = radius / (radius + 0.5)
    low[...] = x_before[...].astype(jnp.float32)
    high[...] = x_after[...].astype(jnp.float32)
    for c in range(3):
        density[...] = deposit(across[...], along[c])
        for t in range(th):
            v = velocity[c, t]
            ahead, behind = axial_neighbours(v, low[c, t : t + 1, :], high[c, t : t + 1, :])
            above = velocity[c, t + 1] if t < th - 1 else theta_after[c].astype(jnp.float32)
            under = velocity[c, t - 1] if t > 0 else theta_before[c].astype(jnp.float32)
            outer, inner = radial_neighbours(v)
            around = (ahead + behind) + (above + under) + (outward * outer + inward * inner)
            out[c, t] = (
                (1.0 - 6.0 * DIFFUSE) * v
                + DIFFUSE * around
                + density[t * ROWS : (t + 1) * ROWS, :]
            )


def transform_body(table, source, out):
    product = jnp.dot(table[...], source[...], preferred_element_type=jnp.float32)
    out[...] = product.astype(jnp.bfloat16)


def solve_body(spread, inverse, out, whole):
    rows = spread.shape[1]
    halves = whole.shape[0]
    for x in range(ROWS):
        for half in range(halves):
            layer = spread[x * halves + half].astype(jnp.float32)
            whole[half, pl.ds(x, rows, stride=ROWS), :] = layer
    group = 2 * ROWS
    for j in range(inverse.shape[0]):
        span = slice(j * group, (j + 1) * group)
        pair = jnp.concatenate([whole[half, span, :] for half in range(halves)], axis=1)
        out[span, :] = lax.dot_general(
            pair.astype(jnp.bfloat16),
            inverse[j],
            (((1,), (1,)), ((), ())),
            preferred_element_type=jnp.float32,
        )


def spectral_table(length):
    row = np.arange(length)[:, None]
    frequency = np.where(row == 1, length // 2, row // 2)
    angle = (frequency * np.arange(length)[None, :] % length) * (2.0 * math.pi / length)
    cosine = (row % 2 == 0) | (row == 1)
    table = np.where(cosine, np.cos(angle), np.sin(angle)) * math.sqrt(2.0 / length)
    return table.astype(jnp.bfloat16)


def ring(axis, step):
    count = lax.axis_size(axis)
    return [(i, (i + step) % count) for i in range(count)]


def on_device(
    velocity,
    bubble_slip,
    bubble_size,
    bubble_growth,
    bubble_tile,
    bubble_lane,
    send_counts,
    bubble_order,
    radial_inverse,
):
    _, th, ax, width = velocity.shape
    peers = send_counts.shape[1]
    bubbles = bubble_order.shape[1]
    lines = bubbles // LANES
    groups = lax.axis_size("az")
    f32, bf16 = jnp.float32, jnp.bfloat16
    struct = jax.ShapeDtypeStruct
    square = (lines, LANES)

    packed = call(
        pack_body,
        "pack_bubbles",
        struct((peers, ROWS, LANES), bf16),
        (
            bubble_slip,
            bubble_size.reshape(square),
            bubble_growth.reshape(square),
            bubble_tile.reshape(square),
            bubble_lane.reshape(square),
            send_counts,
            bubble_order,
        ),
        scratch=(
            pltpu.VMEM(square, jnp.int32),
            pltpu.VMEM((3,) + square, f32),
            pltpu.VMEM((5,) + square, f32),
            pltpu.VMEM((peers, ROWS, LANES), f32),
        ),
    )
    arrived = lax.all_to_all(packed, "ax", split_axis=0, concat_axis=0, tiled=True)

    first_theta, last_theta, first_x, last_x = call(
        edges_body,
        "edge_layers",
        (
            struct((3, ax, width), bf16),
            struct((3, ax, width), bf16),
            struct((3, th, width), bf16),
            struct((3, th, width), bf16),
        ),
        (velocity, packed),
        specs=[VMEM, ANY],
    )
    theta_before = lax.ppermute(last_theta, "az", ring("az", 1))
    theta_after = lax.ppermute(first_theta, "az", ring("az", -1))
    x_before = lax.ppermute(last_x, "ax", ring("ax", 1))
    x_after = lax.ppermute(first_x, "ax", ring("ax", -1))
    divergence = call(
        divergence_body,
        "divergence",
        struct((th, ax, width), f32),
        (velocity, theta_before, theta_after, x_before, x_after),
        scratch=(pltpu.VMEM((th, width), f32), pltpu.VMEM((th, width), f32)),
    )

    slots = peers * LANES
    cells = th * ax
    source = call(
        source_body,
        "source",
        struct((groups, th, LANES), bf16),
        (arrived, divergence),
        scratch=(
            pltpu.VMEM((cells, slots), bf16),
            pltpu.VMEM((1, width, slots), bf16),
            pltpu.VMEM((width // LANES, cells, LANES), f32),
        ),
        flops=2 * cells * slots * width,
    )
    gathered = lax.all_to_all(source, "az", split_axis=0, concat_axis=0, tiled=True)

    predicted = call(
        predictor_body,
        "predictor",
        struct(velocity.shape, f32),
        (arrived, velocity, theta_before, theta_after, x_before, x_after),
        scratch=(
            pltpu.VMEM((cells, slots), bf16),
            pltpu.VMEM((3, width, slots), bf16),
            pltpu.VMEM((3, th, width), f32),
            pltpu.VMEM((3, th, width), f32),
            pltpu.VMEM((cells, width), f32),
        ),
        flops=2 * 3 * cells * slots * width,
        limit=32,
    )

    length = groups * th
    table = jnp.asarray(spectral_table(length))
    coefficients = call(
        transform_body,
        "transform",
        struct((length, LANES), bf16),
        (table, gathered.reshape(length, LANES)),
        flops=2 * length * length * LANES,
    )
    spread = lax.all_to_all(
        coefficients.reshape(groups, th, LANES), "az", split_axis=0, concat_axis=0, tiled=True
    )
    modes = call(
        solve_body,
        "solve",
        struct((th * ax, width), f32),
        (spread, radial_inverse),
        scratch=(pltpu.VMEM((width // LANES, th * ax, LANES), f32),),
        flops=2 * th * ax * width * width,
    )
    return predicted, modes.reshape(th, ax, width)


def solution(mesh):
    placed = (
        P(None, "az", "ax", None),
        P(None, ("az", "ax")),
        P(("az", "ax")),
        P(("az", "ax")),
        P(("az", "ax")),
        P(("az", "ax")),
        P(("az", "ax"), None),
        P(("az", "ax"), None),
        P("az", None, None),
    )
    return jax.shard_map(
        on_device,
        mesh=mesh,
        in_specs=placed,
        out_specs=(P(None, "az", "ax", None), P("az", "ax", None)),
        check_vma=False,
    )
```

```python
import functools
import math

import jax
import jax.numpy as jnp
import numpy as np
from jax import lax
from jax.experimental import pallas as pl
from jax.experimental.pallas import tpu as pltpu
from jax.sharding import PartitionSpec as P

DIFFUSE = 0.12
LANES = 128
ROWS = 8

VMEM = pl.BlockSpec(memory_space=pltpu.VMEM)
ANY = pl.BlockSpec(memory_space=pl.ANY)


def call(body, name, out_shape, operands, scratch=(), specs=None, flops=0, limit=24):
    moved = sum(x.size * x.dtype.itemsize for x in operands)
    return pl.pallas_call(
        body,
        name=name,
        out_shape=out_shape,
        in_specs=[VMEM] * len(operands) if specs is None else specs,
        out_specs=jax.tree.map(lambda _: VMEM, out_shape),
        scratch_shapes=list(scratch),
        compiler_params=pltpu.CompilerParams(vmem_limit_bytes=limit * 1024 * 1024),
        cost_estimate=pl.CostEstimate(flops=flops, bytes_accessed=moved, transcendentals=0),
    )(*operands)


def take_rows(table, row, lane, shape):
    found = jnp.zeros(shape, table.dtype)
    for r in range(table.shape[0]):
        line = jnp.broadcast_to(table[r : r + 1, :], shape)
        picked = jnp.take_along_axis(line, lane, axis=1, mode="promise_in_bounds")
        found = jnp.where(row == r, picked, found)
    return found


def pack_body(*refs):
    hbm, (out, first_x, last_x), held = refs[:8], refs[8:11], refs[11:19]
    listed, slips, payload, staged, sems = refs[19:]
    copies = [
        pltpu.make_async_copy(source, target, sems.at[i])
        for i, (source, target) in enumerate(zip(hbm, held))
    ]
    for copy in copies:
        copy.start()
    for copy in copies[:7]:
        copy.wait()
    slip, size, growth, tile, lane, counts, order, block = held
    lines = listed.shape[0]
    peers = counts.shape[1]
    for j in range(lines):
        span = slice(j * LANES, (j + 1) * LANES)
        listed[j : j + 1, :] = order[0:1, span]
        for k in range(3):
            slips[k, j : j + 1, :] = slip[k : k + 1, span]
    s0, s1, s2 = slips[0], slips[1], slips[2]
    scale = size[...] * jnp.sqrt(1.0 + s0 * s0 + s1 * s1 + s2 * s2)
    payload[0] = scale * s0
    payload[1] = scale * s1
    payload[2] = scale * s2
    payload[3] = size[...] * growth[...]
    payload[4] = (tile[...] * LANES + lane[...]).astype(jnp.float32)
    count_rows = jnp.broadcast_to(counts[...], (peers, peers))
    below = lax.broadcasted_iota(jnp.int32, (peers, peers), 1) < lax.broadcasted_iota(
        jnp.int32, (peers, peers), 0
    )
    own = lax.broadcasted_iota(jnp.int32, (peers, peers), 1) == lax.broadcasted_iota(
        jnp.int32, (peers, peers), 0
    )
    start = jnp.sum(jnp.where(below, count_rows, 0), axis=1, keepdims=True)
    count = jnp.sum(jnp.where(own, count_rows, 0), axis=1, keepdims=True)
    shape = (peers, LANES)
    slot = lax.broadcasted_iota(jnp.int32, shape, 1)
    used = slot < count
    place = jnp.minimum(start + slot, lines * LANES - 1)
    bubble = take_rows(listed, place >> 7, place & 127, shape)
    row, column = bubble >> 7, bubble & 127
    for k in range(4):
        value = take_rows(payload.at[k], row, column, shape)
        staged[:, k, :] = jnp.where(used, value, 0.0)
    cell = take_rows(payload.at[4], row, column, shape).astype(jnp.int32)
    cell = jnp.where(used, cell, 0)
    staged[:, 4, :] = (cell >> 8).astype(jnp.float32)
    staged[:, 5, :] = (cell & 255).astype(jnp.float32)
    staged[:, 6, :] = jnp.zeros(shape, jnp.float32)
    staged[:, 7, :] = jnp.zeros(shape, jnp.float32)
    out[...] = staged[...].astype(jnp.bfloat16)
    copies[7].wait()
    first_x[...] = block[:, :, 0, :].astype(jnp.bfloat16)
    last_x[...] = block[:, :, ROWS - 1, :].astype(jnp.bfloat16)


def radial_neighbours(v):
    column = lax.broadcasted_iota(jnp.int32, v.shape, 1)
    last = v.shape[1] - 1
    outer = jnp.where(column == last, 0.0, pltpu.roll(v, last, 1))
    inner = jnp.where(column == 0, 0.0, pltpu.roll(v, 1, 1))
    return outer, inner


def axial_neighbours(v, before, after):
    row = lax.broadcasted_iota(jnp.int32, v.shape, 0)
    ahead = jnp.where(row == ROWS - 1, after, pltpu.roll(v, ROWS - 1, 0))
    behind = jnp.where(row == 0, before, pltpu.roll(v, 1, 0))
    return ahead, behind


def interior_body(
    velocity, _, first_theta, last_theta, divergence, held, sems
):
    th, width = held.shape[1], held.shape[3]
    parts = sems.shape[1]
    step = th // parts
    copies = []
    for c in range(3):
        for p in range(parts):
            span = (c, pl.ds(p * step, step))
            copies.append(pltpu.make_async_copy(velocity.at[span], held.at[span], sems.at[c, p]))
    for copy in copies:
        copy.start()
    for copy in copies:
        copy.wait()
    first_theta[...] = held[:, 0].astype(jnp.bfloat16)
    last_theta[...] = held[:, th - 1].astype(jnp.bfloat16)
    radius = lax.broadcasted_iota(jnp.int32, (ROWS, width), 1).astype(jnp.float32)
    outward = (radius + 1.0) / (2.0 * radius + 1.0)
    inward = radius / (2.0 * radius + 1.0)
    for t in range(th):
        ahead, behind = axial_neighbours(held[0, t], 0.0, 0.0)
        around = ahead - behind
        if t < th - 1:
            around = around + held[1, t + 1]
        if t > 0:
            around = around - held[1, t - 1]
        outer, inner = radial_neighbours(held[2, t])
        divergence[t] = 0.5 * around + (outward * outer - inward * inner)


def after(arrays, event):
    count = len(arrays)
    return pl.pallas_call(
        lambda *refs: None,
        name="after",
        out_shape=tuple(jax.ShapeDtypeStruct(x.shape, x.dtype) for x in arrays),
        in_specs=[ANY] * (count + 1),
        out_specs=(ANY,) * count,
        input_output_aliases={i: i for i in range(count)},
        compiler_params=pltpu.CompilerParams(vmem_limit_bytes=60 * 1024 * 1024),
    )(*arrays, event)


def cell_hot(index_line, cells):
    row = lax.broadcasted_iota(jnp.int32, (cells, LANES), 0).astype(jnp.bfloat16)
    return row == jnp.broadcast_to(index_line, (cells, LANES))


def hot_parts(arrived, first, count, across, along):
    cells = across.shape[0]
    zero = jnp.zeros((cells, LANES), jnp.bfloat16)
    for h in range(arrived.shape[0]):
        span = slice(h * LANES, (h + 1) * LANES)
        block = arrived[h]
        across[:, span] = jnp.where(cell_hot(block[4:5, :], cells), jnp.ones_like(zero), zero)
        here = cell_hot(block[5:6, :], cells)
        for k in range(count):
            value = jnp.broadcast_to(block[first + k : first + k + 1, :], zero.shape)
            along[k, :, span] = jnp.where(here, value, zero)


def deposit(across, along):
    return lax.dot_general(
        across, along, (((1,), (1,)), ((), ())), preferred_element_type=jnp.float32
    )


def source_body(
    arrived, divergence, x_before, x_after, first_theta, last_theta, out, across, along, whole
):
    th = divergence.shape[0]
    hot_parts(arrived, 3, 1, across, along)
    density = deposit(across[...], along[0])
    total = density + divergence[...].reshape(density.shape)
    halves = whole.shape[0]
    blank = jnp.zeros((out.shape[1] - th - 2, LANES), jnp.float32)
    first = first_theta[1].astype(jnp.float32)
    last = last_theta[1].astype(jnp.float32)
    for half in range(halves):
        span = slice(half * LANES, (half + 1) * LANES)
        whole[half] = total[:, span]
        for x in range(ROWS):
            layer = whole[half, pl.ds(x, th, stride=ROWS), :]
            if x == 0:
                layer = layer - 0.5 * x_before[0, :, span].astype(jnp.float32)
            if x == ROWS - 1:
                layer = layer + 0.5 * x_after[0, :, span].astype(jnp.float32)
            edges = [first[x : x + 1, span], last[x : x + 1, span], blank]
            column = jnp.concatenate([layer] + edges, axis=0)
            out[x * halves + half] = column.astype(jnp.bfloat16)


def predictor_body(
    arrived, velocity, theta_before, theta_after, x_before, x_after, out, across, along, low, high,
    density,
):
    th, width = velocity.shape[1], velocity.shape[3]
    hot_parts(arrived, 0, 3, across, along)
    radius = lax.broadcasted_iota(jnp.int32, (ROWS, width), 1).astype(jnp.float32)
    outward = (radius + 1.0) / (radius + 0.5)
    inward = radius / (radius + 0.5)
    low[...] = x_before[...].astype(jnp.float32)
    high[...] = x_after[...].astype(jnp.float32)
    for c in range(3):
        density[...] = deposit(across[...], along[c])
        for t in range(th):
            v = velocity[c, t]
            ahead, behind = axial_neighbours(v, low[c, t : t + 1, :], high[c, t : t + 1, :])
            above = velocity[c, t + 1] if t < th - 1 else theta_after[c].astype(jnp.float32)
            under = velocity[c, t - 1] if t > 0 else theta_before[c].astype(jnp.float32)
            outer, inner = radial_neighbours(v)
            around = (ahead + behind) + (above + under) + (outward * outer + inward * inner)
            out[c, t] = (
                (1.0 - 6.0 * DIFFUSE) * v
                + DIFFUSE * around
                + density[t * ROWS : (t + 1) * ROWS, :]
            )


def transform_body(table, source, before, after, out):
    product = jnp.dot(table[...], source[...], preferred_element_type=jnp.float32)
    out[...] = product.astype(jnp.bfloat16)


def solve_body(spread, inverse, out, whole):
    rows = spread.shape[1]
    halves = whole.shape[0]
    for x in range(ROWS):
        for half in range(halves):
            layer = spread[x * halves + half].astype(jnp.float32)
            whole[half, pl.ds(x, rows, stride=ROWS), :] = layer
    group = 2 * ROWS
    for j in range(inverse.shape[0]):
        span = slice(j * group, (j + 1) * group)
        pair = jnp.concatenate([whole[half, span, :] for half in range(halves)], axis=1)
        out[span, :] = lax.dot_general(
            pair.astype(jnp.bfloat16),
            inverse[j],
            (((1,), (1,)), ((), ())),
            preferred_element_type=jnp.float32,
        )


def spectral_table(length, blocks, extra):
    row = np.arange(length)[:, None]
    frequency = np.where(row == 1, length // 2, row // 2)
    angle = (frequency * np.arange(length)[None, :] % length) * (2.0 * math.pi / length)
    cosine = (row % 2 == 0) | (row == 1)
    table = np.where(cosine, np.cos(angle), np.sin(angle)) * math.sqrt(2.0 / length)
    step = length // blocks
    wide = np.zeros((length, blocks, step + extra))
    wide[:, :, :step] = table.reshape(length, blocks, step)
    starts = np.arange(blocks) * step
    wide[:, :, step] = 0.5 * table[:, (starts - 1) % length]
    wide[:, :, step + 1] = -0.5 * table[:, (starts + step) % length]
    return wide.reshape(length, -1).astype(jnp.bfloat16)


def ring(axis, step):
    count = lax.axis_size(axis)
    return [(i, (i + step) % count) for i in range(count)]


def on_device(
    velocity,
    bubble_slip,
    bubble_size,
    bubble_growth,
    bubble_tile,
    bubble_lane,
    send_counts,
    bubble_order,
    radial_inverse,
):
    _, th, ax, width = velocity.shape
    peers = send_counts.shape[1]
    bubbles = bubble_order.shape[1]
    lines = bubbles // LANES
    groups = lax.axis_size("az")
    f32, bf16 = jnp.float32, jnp.bfloat16
    struct = jax.ShapeDtypeStruct
    square = (lines, LANES)

    bubbles_in = (
        bubble_slip,
        bubble_size.reshape(square),
        bubble_growth.reshape(square),
        bubble_tile.reshape(square),
        bubble_lane.reshape(square),
        send_counts,
        bubble_order,
    )
    bubbles_in = bubbles_in + (velocity,)
    packed, first_x, last_x = call(
        pack_body,
        "pack_bubbles",
        (
            struct((peers, ROWS, LANES), bf16),
            struct((3, th, width), bf16),
            struct((3, th, width), bf16),
        ),
        bubbles_in,
        specs=[ANY] * 8,
        limit=60,
        scratch=tuple(pltpu.VMEM(x.shape, x.dtype) for x in bubbles_in)
        + (
            pltpu.VMEM(square, jnp.int32),
            pltpu.VMEM((3,) + square, f32),
            pltpu.VMEM((5,) + square, f32),
            pltpu.VMEM((peers, ROWS, LANES), f32),
            pltpu.SemaphoreType.DMA((8,)),
        ),
    )
    arrived = lax.all_to_all(packed, "ax", split_axis=0, concat_axis=0, tiled=True)

    first_x, last_x = after((first_x, last_x), packed)
    x_before = lax.ppermute(last_x, "ax", ring("ax", 1))
    x_after = lax.ppermute(first_x, "ax", ring("ax", -1))
    first_theta, last_theta, divergence = call(
        interior_body,
        "interior",
        (
            struct((3, ax, width), bf16),
            struct((3, ax, width), bf16),
            struct((th, ax, width), f32),
        ),
        (velocity, packed),
        specs=[ANY, ANY],
        scratch=(pltpu.VMEM(velocity.shape, f32), pltpu.SemaphoreType.DMA((3, 2))),
    )

    slots = peers * LANES
    cells = th * ax
    extra = 8
    source = call(
        source_body,
        "source",
        struct((groups, th + extra, LANES), bf16),
        (arrived, divergence, x_before, x_after, first_theta, last_theta),
        scratch=(
            pltpu.VMEM((cells, slots), bf16),
            pltpu.VMEM((1, width, slots), bf16),
            pltpu.VMEM((width // LANES, cells, LANES), f32),
        ),
        flops=2 * cells * slots * width,
    )
    gathered = lax.all_to_all(source, "az", split_axis=0, concat_axis=0, tiled=True)

    first_layer, last_layer = after((first_theta, last_theta), source)
    theta_before = lax.ppermute(last_layer, "az", ring("az", 1))
    theta_after = lax.ppermute(first_layer, "az", ring("az", -1))

    predicted = call(
        predictor_body,
        "predictor",
        struct(velocity.shape, f32),
        (arrived, velocity, theta_before, theta_after, x_before, x_after),
        scratch=(
            pltpu.VMEM((cells, slots), bf16),
            pltpu.VMEM((3, width, slots), bf16),
            pltpu.VMEM((3, th, width), f32),
            pltpu.VMEM((3, th, width), f32),
            pltpu.VMEM((cells, width), f32),
        ),
        flops=2 * 3 * cells * slots * width,
        limit=32,
    )

    length = groups * th
    table = jnp.asarray(spectral_table(length, groups, extra))
    coefficients = call(
        transform_body,
        "transform",
        struct((length, LANES), bf16),
        (table, gathered.reshape(-1, LANES), theta_before, theta_after),
        specs=[VMEM, VMEM, ANY, ANY],
        flops=2 * length * (length + groups * extra) * LANES,
    )
    spread = lax.all_to_all(
        coefficients.reshape(groups, th, LANES), "az", split_axis=0, concat_axis=0, tiled=True
    )
    modes = call(
        solve_body,
        "solve",
        struct((th * ax, width), f32),
        (spread, radial_inverse),
        scratch=(pltpu.VMEM((width // LANES, th * ax, LANES), f32),),
        flops=2 * th * ax * width * width,
    )
    return predicted, modes.reshape(th, ax, width)


def solution(mesh):
    placed = (
        P(None, "az", "ax", None),
        P(None, ("az", "ax")),
        P(("az", "ax")),
        P(("az", "ax")),
        P(("az", "ax")),
        P(("az", "ax")),
        P(("az", "ax"), None),
        P(("az", "ax"), None),
        P("az", None, None),
    )
    return jax.shard_map(
        on_device,
        mesh=mesh,
        in_specs=placed,
        out_specs=(P(None, "az", "ax", None), P("az", "ax", None)),
        check_vma=False,
    )
```

```python
import functools
import math

import jax
import jax.numpy as jnp
import numpy as np
from jax import lax
from jax.experimental import pallas as pl
from jax.experimental.pallas import tpu as pltpu
from jax.sharding import PartitionSpec as P

DIFFUSE = 0.12
LANES = 128
ROWS = 8

VMEM = pl.BlockSpec(memory_space=pltpu.VMEM)
ANY = pl.BlockSpec(memory_space=pl.ANY)


def call(
    body, name, out_shape, operands, scratch=(), specs=None, flops=0, limit=24, out_specs=None,
    aliases=None,
):
    moved = sum(x.size * x.dtype.itemsize for x in operands)
    return pl.pallas_call(
        body,
        name=name,
        out_shape=out_shape,
        in_specs=[VMEM] * len(operands) if specs is None else specs,
        out_specs=jax.tree.map(lambda _: VMEM, out_shape) if out_specs is None else out_specs,
        input_output_aliases=aliases or {},
        scratch_shapes=list(scratch),
        compiler_params=pltpu.CompilerParams(vmem_limit_bytes=limit * 1024 * 1024),
        cost_estimate=pl.CostEstimate(flops=flops, bytes_accessed=moved, transcendentals=0),
    )(*operands)


def take_rows(table, row, lane, shape):
    found = jnp.zeros(shape, table.dtype)
    for r in range(table.shape[0]):
        line = jnp.broadcast_to(table[r : r + 1, :], shape)
        picked = jnp.take_along_axis(line, lane, axis=1, mode="promise_in_bounds")
        found = jnp.where(row == r, picked, found)
    return found


def pack_body(*refs):
    hbm, held = refs[:8], refs[13:21]
    out, first_x, last_x, first_theta, last_theta = refs[8:13]
    listed, slips, payload, staged, sems = refs[21:]
    copies = [
        pltpu.make_async_copy(source, target, sems.at[i])
        for i, (source, target) in enumerate(zip(hbm, held))
    ]
    for copy in copies:
        copy.start()
    for copy in copies[:7]:
        copy.wait()
    slip, size, growth, tile, lane, counts, order, block = held
    lines = listed.shape[0]
    peers = counts.shape[1]
    for j in range(lines):
        span = slice(j * LANES, (j + 1) * LANES)
        listed[j : j + 1, :] = order[0:1, span]
        for k in range(3):
            slips[k, j : j + 1, :] = slip[k : k + 1, span]
    s0, s1, s2 = slips[0], slips[1], slips[2]
    scale = size[...] * jnp.sqrt(1.0 + s0 * s0 + s1 * s1 + s2 * s2)
    payload[0] = scale * s0
    payload[1] = scale * s1
    payload[2] = scale * s2
    payload[3] = size[...] * growth[...]
    payload[4] = (tile[...] * LANES + lane[...]).astype(jnp.float32)
    count_rows = jnp.broadcast_to(counts[...], (peers, peers))
    below = lax.broadcasted_iota(jnp.int32, (peers, peers), 1) < lax.broadcasted_iota(
        jnp.int32, (peers, peers), 0
    )
    own = lax.broadcasted_iota(jnp.int32, (peers, peers), 1) == lax.broadcasted_iota(
        jnp.int32, (peers, peers), 0
    )
    start = jnp.sum(jnp.where(below, count_rows, 0), axis=1, keepdims=True)
    count = jnp.sum(jnp.where(own, count_rows, 0), axis=1, keepdims=True)
    shape = (peers, LANES)
    slot = lax.broadcasted_iota(jnp.int32, shape, 1)
    used = slot < count
    place = jnp.minimum(start + slot, lines * LANES - 1)
    bubble = take_rows(listed, place >> 7, place & 127, shape)
    row, column = bubble >> 7, bubble & 127
    for k in range(4):
        value = take_rows(payload.at[k], row, column, shape)
        staged[:, k, :] = jnp.where(used, value, 0.0)
    cell = take_rows(payload.at[4], row, column, shape).astype(jnp.int32)
    cell = jnp.where(used, cell, 0)
    staged[:, 4, :] = (cell >> 8).astype(jnp.float32)
    staged[:, 5, :] = (cell & 255).astype(jnp.float32)
    staged[:, 6, :] = jnp.zeros(shape, jnp.float32)
    staged[:, 7, :] = jnp.zeros(shape, jnp.float32)
    out[...] = staged[...].astype(jnp.bfloat16)
    copies[7].wait()
    first_x[...] = block[:, :, 0, :].astype(jnp.bfloat16)
    last_x[...] = block[:, :, ROWS - 1, :].astype(jnp.bfloat16)
    first_theta[...] = block[:, 0].astype(jnp.bfloat16)
    last_theta[...] = block[:, block.shape[1] - 1].astype(jnp.bfloat16)


def radial_neighbours(v):
    column = lax.broadcasted_iota(jnp.int32, v.shape, 1)
    last = v.shape[1] - 1
    outer = jnp.where(column == last, 0.0, pltpu.roll(v, last, 1))
    inner = jnp.where(column == 0, 0.0, pltpu.roll(v, 1, 1))
    return outer, inner


def axial_neighbours(v, before, after):
    row = lax.broadcasted_iota(jnp.int32, v.shape, 0)
    ahead = jnp.where(row == ROWS - 1, after, pltpu.roll(v, ROWS - 1, 0))
    behind = jnp.where(row == 0, before, pltpu.roll(v, 1, 0))
    return ahead, behind


def after(arrays, event):
    count = len(arrays)
    return pl.pallas_call(
        lambda *refs: None,
        name="after",
        out_shape=tuple(jax.ShapeDtypeStruct(x.shape, x.dtype) for x in arrays),
        in_specs=[ANY] * (count + 1),
        out_specs=(ANY,) * count,
        input_output_aliases={i: i for i in range(count)},
        compiler_params=pltpu.CompilerParams(vmem_limit_bytes=60 * 1024 * 1024),
    )(*arrays, event)


def cell_hot(index_line, cells):
    row = lax.broadcasted_iota(jnp.int32, (cells, LANES), 0).astype(jnp.bfloat16)
    return row == jnp.broadcast_to(index_line, (cells, LANES))


def hot_parts(arrived, first, count, across, along):
    cells = across.shape[0]
    zero = jnp.zeros((cells, LANES), jnp.bfloat16)
    for h in range(arrived.shape[0]):
        span = slice(h * LANES, (h + 1) * LANES)
        block = arrived[h]
        across[:, span] = jnp.where(cell_hot(block[4:5, :], cells), jnp.ones_like(zero), zero)
        here = cell_hot(block[5:6, :], cells)
        for k in range(count):
            value = jnp.broadcast_to(block[first + k : first + k + 1, :], zero.shape)
            along[k, :, span] = jnp.where(here, value, zero)


def deposit(across, along):
    return lax.dot_general(
        across, along, (((1,), (1,)), ((), ())), preferred_element_type=jnp.float32
    )


def partial_body(
    arrived, velocity, out, edges, across, along, total, whole
):
    hot_parts(arrived, 3, 1, across, along)
    density = deposit(across[...], along[0])
    th, width = velocity.shape[1], velocity.shape[3]
    radius = lax.broadcasted_iota(jnp.int32, (ROWS, width), 1).astype(jnp.float32)
    outward = (radius + 1.0) / (2.0 * radius + 1.0)
    inward = radius / (2.0 * radius + 1.0)
    for t in range(th):
        ahead, behind = axial_neighbours(velocity[0, t], 0.0, 0.0)
        around = ahead - behind
        if t < th - 1:
            around = around + velocity[1, t + 1]
        if t > 0:
            around = around - velocity[1, t - 1]
        outer, inner = radial_neighbours(velocity[2, t])
        total[t * ROWS : (t + 1) * ROWS, :] = 0.5 * around + (outward * outer - inward * inner)
    halves = whole.shape[0]
    blank = jnp.zeros((out.shape[1] - th - 2, LANES), jnp.float32)
    first = velocity[1, 0]
    last = velocity[1, th - 1]
    for half in range(halves):
        span = slice(half * LANES, (half + 1) * LANES)
        whole[half] = density[:, span] + total[:, span]
        for x in range(ROWS):
            layer = whole[half, pl.ds(x, th, stride=ROWS), :]
            ends = [first[x : x + 1, span], last[x : x + 1, span], blank]
            column = jnp.concatenate([layer] + ends, axis=0)
            out[x * halves + half] = column.astype(jnp.bfloat16)
            if x == 0:
                edges[half] = column
            if x == ROWS - 1:
                edges[halves + half] = column


def complete_body(_, edges, x_before, x_after, out, staged, sems):
    groups, th = out.shape[0], x_before.shape[1]
    halves = edges.shape[0] // 2
    for half in range(halves):
        span = slice(half * LANES, (half + 1) * LANES)
        before = 0.5 * x_before[0, :, span].astype(jnp.float32)
        beyond = 0.5 * x_after[0, :, span].astype(jnp.float32)
        blank = jnp.zeros((edges.shape[1] - th, LANES), jnp.float32)
        low = edges[half] - jnp.concatenate([before, blank], axis=0)
        high = edges[halves + half] + jnp.concatenate([beyond, blank], axis=0)
        staged[half] = low.astype(jnp.bfloat16)
        staged[halves + half] = high.astype(jnp.bfloat16)
    copies = [
        pltpu.make_async_copy(
            staged.at[pl.ds(i * halves, halves)],
            out.at[pl.ds(i * (groups - halves), halves)],
            sems.at[i],
        )
        for i in range(2)
    ]
    for copy in copies:
        copy.start()
    for copy in copies:
        copy.wait()


def predictor_body(*refs):
    hbm, out, held = refs[:6], refs[6], refs[7:13]
    across, along, low, high, density, sems = refs[13:]
    arrived, velocity, theta_before, theta_after, x_before, x_after = held
    copies = [
        pltpu.make_async_copy(source, target, sems.at[i])
        for i, (source, target) in enumerate(zip(hbm, held))
    ]
    for copy in copies:
        copy.start()
    copies[0].wait()
    th, width = velocity.shape[1], velocity.shape[3]
    hot_parts(arrived, 0, 3, across, along)
    for copy in copies[1:]:
        copy.wait()
    radius = lax.broadcasted_iota(jnp.int32, (ROWS, width), 1).astype(jnp.float32)
    outward = (radius + 1.0) / (radius + 0.5)
    inward = radius / (radius + 0.5)
    low[...] = x_before[...].astype(jnp.float32)
    high[...] = x_after[...].astype(jnp.float32)
    for c in range(3):
        density[...] = deposit(across[...], along[c])
        for t in range(th):
            v = velocity[c, t]
            ahead, behind = axial_neighbours(v, low[c, t : t + 1, :], high[c, t : t + 1, :])
            above = velocity[c, t + 1] if t < th - 1 else theta_after[c].astype(jnp.float32)
            under = velocity[c, t - 1] if t > 0 else theta_before[c].astype(jnp.float32)
            outer, inner = radial_neighbours(v)
            around = (ahead + behind) + (above + under) + (outward * outer + inward * inner)
            out[c, t] = (
                (1.0 - 6.0 * DIFFUSE) * v
                + DIFFUSE * around
                + density[t * ROWS : (t + 1) * ROWS, :]
            )


def transform_body(table, source, before, after, out):
    product = jnp.dot(table[...], source[...], preferred_element_type=jnp.float32)
    out[...] = product.astype(jnp.bfloat16)


def solve_body(spread, inverse, out, whole):
    rows = spread.shape[1]
    halves = whole.shape[0]
    for x in range(ROWS):
        for half in range(halves):
            layer = spread[x * halves + half].astype(jnp.float32)
            whole[half, pl.ds(x, rows, stride=ROWS), :] = layer
    group = 2 * ROWS
    for j in range(inverse.shape[0]):
        span = slice(j * group, (j + 1) * group)
        pair = jnp.concatenate([whole[half, span, :] for half in range(halves)], axis=1)
        out[span, :] = lax.dot_general(
            pair.astype(jnp.bfloat16),
            inverse[j],
            (((1,), (1,)), ((), ())),
            preferred_element_type=jnp.float32,
        )


def spectral_table(length, blocks, extra):
    row = np.arange(length)[:, None]
    frequency = np.where(row == 1, length // 2, row // 2)
    angle = (frequency * np.arange(length)[None, :] % length) * (2.0 * math.pi / length)
    cosine = (row % 2 == 0) | (row == 1)
    table = np.where(cosine, np.cos(angle), np.sin(angle)) * math.sqrt(2.0 / length)
    step = length // blocks
    wide = np.zeros((length, blocks, step + extra))
    wide[:, :, :step] = table.reshape(length, blocks, step)
    starts = np.arange(blocks) * step
    wide[:, :, step] = 0.5 * table[:, (starts - 1) % length]
    wide[:, :, step + 1] = -0.5 * table[:, (starts + step) % length]
    return wide.reshape(length, -1).astype(jnp.bfloat16)


def ring(axis, step):
    count = lax.axis_size(axis)
    return [(i, (i + step) % count) for i in range(count)]


def on_device(
    velocity,
    bubble_slip,
    bubble_size,
    bubble_growth,
    bubble_tile,
    bubble_lane,
    send_counts,
    bubble_order,
    radial_inverse,
):
    _, th, ax, width = velocity.shape
    peers = send_counts.shape[1]
    bubbles = bubble_order.shape[1]
    lines = bubbles // LANES
    groups = lax.axis_size("az")
    f32, bf16 = jnp.float32, jnp.bfloat16
    struct = jax.ShapeDtypeStruct
    square = (lines, LANES)

    bubbles_in = (
        bubble_slip,
        bubble_size.reshape(square),
        bubble_growth.reshape(square),
        bubble_tile.reshape(square),
        bubble_lane.reshape(square),
        send_counts,
        bubble_order,
    )
    bubbles_in = bubbles_in + (velocity,)
    packed, first_x, last_x, first_theta, last_theta = call(
        pack_body,
        "pack_bubbles",
        (
            struct((peers, ROWS, LANES), bf16),
            struct((3, th, width), bf16),
            struct((3, th, width), bf16),
            struct((3, ax, width), bf16),
            struct((3, ax, width), bf16),
        ),
        bubbles_in,
        specs=[ANY] * 8,
        limit=60,
        scratch=tuple(pltpu.VMEM(x.shape, x.dtype) for x in bubbles_in)
        + (
            pltpu.VMEM(square, jnp.int32),
            pltpu.VMEM((3,) + square, f32),
            pltpu.VMEM((5,) + square, f32),
            pltpu.VMEM((peers, ROWS, LANES), f32),
            pltpu.SemaphoreType.DMA((8,)),
        ),
    )
    arrived = lax.all_to_all(packed, "ax", split_axis=0, concat_axis=0, tiled=True)

    x_before = lax.ppermute(last_x, "ax", ring("ax", 1))
    x_after = lax.ppermute(first_x, "ax", ring("ax", -1))
    slots = peers * LANES
    cells = th * ax
    extra = 8
    halves = width // LANES
    partial, edges = call(
        partial_body,
        "partial_source",
        (
            struct((groups, th + extra, LANES), bf16),
            struct((2 * halves, th + extra, LANES), f32),
        ),
        (arrived, velocity),
        scratch=(
            pltpu.VMEM((cells, slots), bf16),
            pltpu.VMEM((1, width, slots), bf16),
            pltpu.VMEM((cells, width), f32),
            pltpu.VMEM((halves, cells, LANES), f32),
        ),
        flops=2 * cells * slots * width,
    )
    source = call(
        complete_body,
        "complete_source",
        struct(partial.shape, bf16),
        (partial, edges, x_before, x_after),
        specs=[ANY, VMEM, VMEM, VMEM],
        out_specs=ANY,
        aliases={0: 0},
        scratch=(
            pltpu.VMEM((2 * halves, th + extra, LANES), bf16),
            pltpu.SemaphoreType.DMA((2,)),
        ),
    )
    gathered = lax.all_to_all(source, "az", split_axis=0, concat_axis=0, tiled=True)

    first_layer, last_layer = after((first_theta, last_theta), source)
    theta_before = lax.ppermute(last_layer, "az", ring("az", 1))
    theta_after = lax.ppermute(first_layer, "az", ring("az", -1))

    beside = (arrived, velocity, theta_before, theta_after, x_before, x_after)
    predicted = call(
        predictor_body,
        "predictor",
        struct(velocity.shape, f32),
        beside,
        specs=[ANY] * 6,
        scratch=tuple(pltpu.VMEM(x.shape, x.dtype) for x in beside)
        + (
            pltpu.VMEM((cells, slots), bf16),
            pltpu.VMEM((3, width, slots), bf16),
            pltpu.VMEM((3, th, width), f32),
            pltpu.VMEM((3, th, width), f32),
            pltpu.VMEM((cells, width), f32),
            pltpu.SemaphoreType.DMA((6,)),
        ),
        flops=2 * 3 * cells * slots * width,
        limit=56,
    )

    length = groups * th
    table = jnp.asarray(spectral_table(length, groups, extra))
    coefficients = call(
        transform_body,
        "transform",
        struct((length, LANES), bf16),
        (table, gathered.reshape(-1, LANES), theta_before, theta_after),
        specs=[VMEM, VMEM, ANY, ANY],
        flops=2 * length * (length + groups * extra) * LANES,
    )
    spread = lax.all_to_all(
        coefficients.reshape(groups, th, LANES), "az", split_axis=0, concat_axis=0, tiled=True
    )
    modes = call(
        solve_body,
        "solve",
        struct((th * ax, width), f32),
        (spread, radial_inverse),
        scratch=(pltpu.VMEM((width // LANES, th * ax, LANES), f32),),
        flops=2 * th * ax * width * width,
    )
    return predicted, modes.reshape(th, ax, width)


def solution(mesh):
    placed = (
        P(None, "az", "ax", None),
        P(None, ("az", "ax")),
        P(("az", "ax")),
        P(("az", "ax")),
        P(("az", "ax")),
        P(("az", "ax")),
        P(("az", "ax"), None),
        P(("az", "ax"), None),
        P("az", None, None),
    )
    return jax.shard_map(
        on_device,
        mesh=mesh,
        in_specs=placed,
        out_specs=(P(None, "az", "ax", None), P("az", "ax", None)),
        check_vma=False,
    )
```

```python
import functools
import math

import jax
import jax.numpy as jnp
import numpy as np
from jax import lax
from jax.experimental import pallas as pl
from jax.experimental.pallas import tpu as pltpu
from jax.sharding import PartitionSpec as P

DIFFUSE = 0.12
LANES = 128
ROWS = 8

VMEM = pl.BlockSpec(memory_space=pltpu.VMEM)
ANY = pl.BlockSpec(memory_space=pl.ANY)


def call(
    body, name, out_shape, operands, scratch=(), specs=None, flops=0, limit=24, out_specs=None,
    aliases=None,
):
    moved = sum(x.size * x.dtype.itemsize for x in operands)
    return pl.pallas_call(
        body,
        name=name,
        out_shape=out_shape,
        in_specs=[VMEM] * len(operands) if specs is None else specs,
        out_specs=jax.tree.map(lambda _: VMEM, out_shape) if out_specs is None else out_specs,
        input_output_aliases=aliases or {},
        scratch_shapes=list(scratch),
        compiler_params=pltpu.CompilerParams(vmem_limit_bytes=limit * 1024 * 1024),
        cost_estimate=pl.CostEstimate(flops=flops, bytes_accessed=moved, transcendentals=0),
    )(*operands)


def take_rows(table, row, lane):
    blocks = []
    for first in range(0, row.shape[0], ROWS):
        span = slice(first, first + ROWS)
        found = None
        for r in range(table.shape[0]):
            line = jnp.broadcast_to(table[r : r + 1, :], (ROWS, LANES))
            picked = jnp.take_along_axis(line, lane[span], axis=1, mode="promise_in_bounds")
            found = picked if found is None else jnp.where(row[span] == r, picked, found)
        blocks.append(found)
    return jnp.concatenate(blocks, axis=0)


def pack_body(*refs):
    hbm, held = refs[:8], refs[13:21]
    out, first_x, last_x, first_theta, last_theta = refs[8:13]
    listed, slips, payload, staged, sems = refs[21:]
    copies = [
        pltpu.make_async_copy(source, target, sems.at[i])
        for i, (source, target) in enumerate(zip(hbm, held))
    ]
    for copy in copies:
        copy.start()
    for copy in copies[:7]:
        copy.wait()
    slip, size, growth, tile, lane, counts, order, block = held
    lines = listed.shape[0]
    peers = counts.shape[1]
    for j in range(lines):
        span = slice(j * LANES, (j + 1) * LANES)
        listed[j : j + 1, :] = order[0:1, span]
        for k in range(3):
            slips[k, j : j + 1, :] = slip[k : k + 1, span]
    s0, s1, s2 = slips[0], slips[1], slips[2]
    scale = size[...] * jnp.sqrt(1.0 + s0 * s0 + s1 * s1 + s2 * s2)
    payload[0] = scale * s0
    payload[1] = scale * s1
    payload[2] = scale * s2
    payload[3] = size[...] * growth[...]
    payload[4] = (tile[...] * LANES + lane[...]).astype(jnp.float32)
    count_rows = jnp.broadcast_to(counts[...], (peers, peers))
    below = lax.broadcasted_iota(jnp.int32, (peers, peers), 1) < lax.broadcasted_iota(
        jnp.int32, (peers, peers), 0
    )
    own = lax.broadcasted_iota(jnp.int32, (peers, peers), 1) == lax.broadcasted_iota(
        jnp.int32, (peers, peers), 0
    )
    start = jnp.sum(jnp.where(below, count_rows, 0), axis=1, keepdims=True)
    count = jnp.sum(jnp.where(own, count_rows, 0), axis=1, keepdims=True)
    shape = (peers, LANES)
    slot = lax.broadcasted_iota(jnp.int32, shape, 1)
    used = slot < count
    place = jnp.minimum(start + slot, lines * LANES - 1)
    bubble = take_rows(listed, place >> 7, place & 127)
    row, column = bubble >> 7, bubble & 127
    for k in range(4):
        value = take_rows(payload.at[k], row, column)
        staged[:, k, :] = jnp.where(used, value, 0.0)
    cell = take_rows(payload.at[4], row, column).astype(jnp.int32)
    cell = jnp.where(used, cell, 0)
    staged[:, 4, :] = (cell >> 8).astype(jnp.float32)
    staged[:, 5, :] = (cell & 255).astype(jnp.float32)
    staged[:, 6, :] = jnp.zeros(shape, jnp.float32)
    staged[:, 7, :] = jnp.zeros(shape, jnp.float32)
    out[...] = staged[...].astype(jnp.bfloat16)
    copies[7].wait()
    first_x[...] = block[:, :, 0, :].astype(jnp.bfloat16)
    last_x[...] = block[:, :, ROWS - 1, :].astype(jnp.bfloat16)
    first_theta[...] = block[:, 0].astype(jnp.bfloat16)
    last_theta[...] = block[:, block.shape[1] - 1].astype(jnp.bfloat16)


def radial_neighbours(v):
    column = lax.broadcasted_iota(jnp.int32, v.shape, 1)
    last = v.shape[1] - 1
    outer = jnp.where(column == last, 0.0, pltpu.roll(v, last, 1))
    inner = jnp.where(column == 0, 0.0, pltpu.roll(v, 1, 1))
    return outer, inner


def axial_neighbours(v, before, after):
    row = lax.broadcasted_iota(jnp.int32, v.shape, 0)
    ahead = jnp.where(row == ROWS - 1, after, pltpu.roll(v, ROWS - 1, 0))
    behind = jnp.where(row == 0, before, pltpu.roll(v, 1, 0))
    return ahead, behind


def after(arrays, event):
    count = len(arrays)
    return pl.pallas_call(
        lambda *refs: None,
        name="after",
        out_shape=tuple(jax.ShapeDtypeStruct(x.shape, x.dtype) for x in arrays),
        in_specs=[ANY] * (count + 1),
        out_specs=(ANY,) * count,
        input_output_aliases={i: i for i in range(count)},
        compiler_params=pltpu.CompilerParams(vmem_limit_bytes=60 * 1024 * 1024),
    )(*arrays, event)


def cell_hot(index_line, cells):
    row = lax.broadcasted_iota(jnp.int32, (cells, LANES), 0).astype(jnp.bfloat16)
    return row == jnp.broadcast_to(index_line, (cells, LANES))


def hot_rows(arrived, holders, cells):
    zero = jnp.zeros((cells, LANES), jnp.bfloat16)
    parts = [
        jnp.where(cell_hot(arrived[h][4:5, :], cells), jnp.ones_like(zero), zero) for h in holders
    ]
    return jnp.concatenate(parts, axis=1)


def hot_columns(arrived, holders, cells, component):
    zero = jnp.zeros((cells, LANES), jnp.bfloat16)
    parts = []
    for h in holders:
        value = jnp.broadcast_to(arrived[h][component : component + 1, :], zero.shape)
        parts.append(jnp.where(cell_hot(arrived[h][5:6, :], cells), value, zero))
    return jnp.concatenate(parts, axis=1)


def deposit(rows, columns):
    return lax.dot_general(
        rows, columns, (((1,), (1,)), ((), ())), preferred_element_type=jnp.float32
    )


def density_body(arrived, out):
    step = 4
    total = None
    for first in range(0, arrived.shape[0], step):
        holders = range(first, first + step)
        part = deposit(
            hot_rows(arrived, holders, out.shape[0]),
            hot_columns(arrived, holders, out.shape[1], 3),
        )
        total = part if total is None else total + part
    out[...] = total


def source_body(density, velocity, x_before, x_after, out, total, whole):
    th, width = velocity.shape[1], velocity.shape[3]
    radius = lax.broadcasted_iota(jnp.int32, (ROWS, width), 1).astype(jnp.float32)
    outward = (radius + 1.0) / (2.0 * radius + 1.0)
    inward = radius / (2.0 * radius + 1.0)
    for t in range(th):
        ahead, behind = axial_neighbours(velocity[0, t], 0.0, 0.0)
        around = ahead - behind
        if t < th - 1:
            around = around + velocity[1, t + 1]
        if t > 0:
            around = around - velocity[1, t - 1]
        outer, inner = radial_neighbours(velocity[2, t])
        span = slice(t * ROWS, (t + 1) * ROWS)
        total[span, :] = 0.5 * around + (outward * outer - inward * inner) + density[span, :]
    halves = whole.shape[0]
    blank = jnp.zeros((out.shape[1] - th - 2, LANES), jnp.float32)
    first = velocity[1, 0]
    last = velocity[1, th - 1]
    for half in range(halves):
        span = slice(half * LANES, (half + 1) * LANES)
        whole[half] = total[:, span]
        for x in range(ROWS):
            layer = whole[half, pl.ds(x, th, stride=ROWS), :]
            if x == 0:
                layer = layer - 0.5 * x_before[0, :, span].astype(jnp.float32)
            if x == ROWS - 1:
                layer = layer + 0.5 * x_after[0, :, span].astype(jnp.float32)
            ends = [first[x : x + 1, span], last[x : x + 1, span], blank]
            column = jnp.concatenate([layer] + ends, axis=0)
            out[x * halves + half] = column.astype(jnp.bfloat16)


def predictor_body(*refs):
    hbm, out, held = refs[:6], refs[6], refs[7:13]
    across, low, high, density, sems = refs[13:]
    arrived, velocity, theta_before, theta_after, x_before, x_after = held
    copies = [
        pltpu.make_async_copy(source, target, sems.at[i])
        for i, (source, target) in enumerate(zip(hbm, held))
    ]
    for copy in copies:
        copy.start()
    copies[0].wait()
    th, width = velocity.shape[1], velocity.shape[3]
    step = 4
    starts = range(0, arrived.shape[0], step)
    cells = density.shape[1]
    for start in starts:
        span = slice(start * LANES, (start + step) * LANES)
        across[:, span] = hot_rows(arrived, range(start, start + step), cells)
    for copy in copies[1:]:
        copy.wait()
    radius = lax.broadcasted_iota(jnp.int32, (ROWS, width), 1).astype(jnp.float32)
    outward = (radius + 1.0) / (radius + 0.5)
    inward = radius / (radius + 0.5)
    low[...] = x_before[...].astype(jnp.float32)
    high[...] = x_after[...].astype(jnp.float32)
    for c in range(3):
        total = None
        for start in starts:
            span = slice(start * LANES, (start + step) * LANES)
            columns = hot_columns(arrived, range(start, start + step), width, c)
            part = deposit(across[:, span], columns)
            total = part if total is None else total + part
        density[c] = total
        for t in range(th):
            v = velocity[c, t]
            ahead, behind = axial_neighbours(v, low[c, t : t + 1, :], high[c, t : t + 1, :])
            above = velocity[c, t + 1] if t < th - 1 else theta_after[c].astype(jnp.float32)
            under = velocity[c, t - 1] if t > 0 else theta_before[c].astype(jnp.float32)
            outer, inner = radial_neighbours(v)
            around = (ahead + behind) + (above + under) + (outward * outer + inward * inner)
            out[c, t] = (
                (1.0 - 6.0 * DIFFUSE) * v
                + DIFFUSE * around
                + density[c, t * ROWS : (t + 1) * ROWS, :]
            )


def in_parts(out, staged, sems, make):
    parts = sems.shape[0]
    rows = out.shape[0] // parts
    copies = []
    for i in range(parts):
        span = pl.ds(i * rows, rows)
        make(i * rows, rows)
        copies.append(pltpu.make_async_copy(staged.at[span], out.at[span], sems.at[i]))
        copies[-1].start()
    for copy in copies:
        copy.wait()


def transform_body(table, source, before, after, out, staged, sems):
    def make(first, rows):
        span = slice(first, first + rows)
        product = jnp.dot(table[span, :], source[...], preferred_element_type=jnp.float32)
        staged[span, :] = product.astype(jnp.bfloat16)

    in_parts(out, staged, sems, make)


def solve_body(spread, inverse, out, whole, staged, sems):
    rows = spread.shape[1]
    halves = whole.shape[0]
    for x in range(ROWS):
        for half in range(halves):
            layer = spread[x * halves + half].astype(jnp.float32)
            whole[half, pl.ds(x, rows, stride=ROWS), :] = layer
    group = 2 * ROWS

    def make(first, rows):
        for j in range(first // group, (first + rows) // group):
            span = slice(j * group, (j + 1) * group)
            pair = jnp.concatenate([whole[half, span, :] for half in range(halves)], axis=1)
            staged[span, :] = lax.dot_general(
                pair.astype(jnp.bfloat16),
                inverse[j],
                (((1,), (1,)), ((), ())),
                preferred_element_type=jnp.float32,
            )

    in_parts(out, staged, sems, make)


def spectral_table(length, blocks, extra):
    row = np.arange(length)[:, None]
    frequency = np.where(row == 1, length // 2, row // 2)
    angle = (frequency * np.arange(length)[None, :] % length) * (2.0 * math.pi / length)
    cosine = (row % 2 == 0) | (row == 1)
    table = np.where(cosine, np.cos(angle), np.sin(angle)) * math.sqrt(2.0 / length)
    step = length // blocks
    wide = np.zeros((length, blocks, step + extra))
    wide[:, :, :step] = table.reshape(length, blocks, step)
    starts = np.arange(blocks) * step
    wide[:, :, step] = 0.5 * table[:, (starts - 1) % length]
    wide[:, :, step + 1] = -0.5 * table[:, (starts + step) % length]
    return wide.reshape(length, -1).astype(jnp.bfloat16)


def ring(axis, step):
    count = lax.axis_size(axis)
    return [(i, (i + step) % count) for i in range(count)]


def on_device(
    velocity,
    bubble_slip,
    bubble_size,
    bubble_growth,
    bubble_tile,
    bubble_lane,
    send_counts,
    bubble_order,
    radial_inverse,
):
    _, th, ax, width = velocity.shape
    peers = send_counts.shape[1]
    bubbles = bubble_order.shape[1]
    lines = bubbles // LANES
    groups = lax.axis_size("az")
    f32, bf16 = jnp.float32, jnp.bfloat16
    struct = jax.ShapeDtypeStruct
    square = (lines, LANES)

    bubbles_in = (
        bubble_slip,
        bubble_size.reshape(square),
        bubble_growth.reshape(square),
        bubble_tile.reshape(square),
        bubble_lane.reshape(square),
        send_counts,
        bubble_order,
    )
    bubbles_in = bubbles_in + (velocity,)
    packed, first_x, last_x, first_theta, last_theta = call(
        pack_body,
        "pack_bubbles",
        (
            struct((peers, ROWS, LANES), bf16),
            struct((3, th, width), bf16),
            struct((3, th, width), bf16),
            struct((3, ax, width), bf16),
            struct((3, ax, width), bf16),
        ),
        bubbles_in,
        specs=[ANY] * 8,
        limit=60,
        scratch=tuple(pltpu.VMEM(x.shape, x.dtype) for x in bubbles_in)
        + (
            pltpu.VMEM(square, jnp.int32),
            pltpu.VMEM((3,) + square, f32),
            pltpu.VMEM((5,) + square, f32),
            pltpu.VMEM((peers, ROWS, LANES), f32),
            pltpu.SemaphoreType.DMA((8,)),
        ),
    )
    arrived = lax.all_to_all(packed, "ax", split_axis=0, concat_axis=0, tiled=True)

    x_before = lax.ppermute(last_x, "ax", ring("ax", 1))
    x_after = lax.ppermute(first_x, "ax", ring("ax", -1))
    slots = peers * LANES
    cells = th * ax
    extra = 8
    halves = width // LANES
    density = call(
        density_body,
        "density",
        struct((cells, width), f32),
        (arrived,),
        flops=2 * cells * slots * width,
    )
    source = call(
        source_body,
        "source",
        struct((groups, th + extra, LANES), bf16),
        (density, velocity, x_before, x_after),
        scratch=(pltpu.VMEM((cells, width), f32), pltpu.VMEM((halves, cells, LANES), f32)),
        flops=30 * cells * width,
    )
    gathered = lax.all_to_all(source, "az", split_axis=0, concat_axis=0, tiled=True)

    first_layer, last_layer = after((first_theta, last_theta), source)
    theta_before = lax.ppermute(last_layer, "az", ring("az", 1))
    theta_after = lax.ppermute(first_layer, "az", ring("az", -1))

    beside = (arrived, velocity, theta_before, theta_after, x_before, x_after)
    predicted = call(
        predictor_body,
        "predictor",
        struct(velocity.shape, f32),
        beside,
        specs=[ANY] * 6,
        scratch=tuple(pltpu.VMEM(x.shape, x.dtype) for x in beside)
        + (
            pltpu.VMEM((cells, slots), bf16),
            pltpu.VMEM((3, th, width), f32),
            pltpu.VMEM((3, th, width), f32),
            pltpu.VMEM((3, cells, width), f32),
            pltpu.SemaphoreType.DMA((6,)),
        ),
        flops=2 * 3 * cells * slots * width,
        limit=56,
    )

    length = groups * th
    table = jnp.asarray(spectral_table(length, groups, extra))
    coefficients = call(
        transform_body,
        "transform",
        struct((length, LANES), bf16),
        (table, gathered.reshape(-1, LANES), theta_before, theta_after),
        specs=[VMEM, VMEM, ANY, ANY],
        out_specs=ANY,
        scratch=(pltpu.VMEM((length, LANES), bf16), pltpu.SemaphoreType.DMA((2,))),
        flops=2 * length * (length + groups * extra) * LANES,
    )
    spread = lax.all_to_all(
        coefficients.reshape(groups, th, LANES), "az", split_axis=0, concat_axis=0, tiled=True
    )
    modes = call(
        solve_body,
        "solve",
        struct((th * ax, width), f32),
        (spread, radial_inverse),
        out_specs=ANY,
        scratch=(
            pltpu.VMEM((halves, cells, LANES), f32),
            pltpu.VMEM((cells, width), f32),
            pltpu.SemaphoreType.DMA((4,)),
        ),
        flops=2 * th * ax * width * width,
    )
    return predicted, modes.reshape(th, ax, width)


def solution(mesh):
    placed = (
        P(None, "az", "ax", None),
        P(None, ("az", "ax")),
        P(("az", "ax")),
        P(("az", "ax")),
        P(("az", "ax")),
        P(("az", "ax")),
        P(("az", "ax"), None),
        P(("az", "ax"), None),
        P("az", None, None),
    )
    return jax.shard_map(
        on_device,
        mesh=mesh,
        in_specs=placed,
        out_specs=(P(None, "az", "ax", None), P("az", "ax", None)),
        check_vma=False,
    )
```

```python
import functools
import math

import jax
import jax.numpy as jnp
import numpy as np
from jax import lax
from jax.experimental import pallas as pl
from jax.experimental.pallas import tpu as pltpu
from jax.sharding import PartitionSpec as P

DIFFUSE = 0.12
LANES = 128
ROWS = 8

VMEM = pl.BlockSpec(memory_space=pltpu.VMEM)
ANY = pl.BlockSpec(memory_space=pl.ANY)


def call(
    body, name, out_shape, operands, scratch=(), specs=None, flops=0, limit=24, out_specs=None,
    aliases=None,
):
    moved = sum(x.size * x.dtype.itemsize for x in operands)
    return pl.pallas_call(
        body,
        name=name,
        out_shape=out_shape,
        in_specs=[VMEM] * len(operands) if specs is None else specs,
        out_specs=jax.tree.map(lambda _: VMEM, out_shape) if out_specs is None else out_specs,
        input_output_aliases=aliases or {},
        scratch_shapes=list(scratch),
        compiler_params=pltpu.CompilerParams(vmem_limit_bytes=limit * 1024 * 1024),
        cost_estimate=pl.CostEstimate(flops=flops, bytes_accessed=moved, transcendentals=0),
    )(*operands)


def take_rows(table, row, lane):
    blocks = []
    for first in range(0, row.shape[0], ROWS):
        span = slice(first, first + ROWS)
        found = None
        for r in range(table.shape[0]):
            line = jnp.broadcast_to(table[r : r + 1, :], (ROWS, LANES))
            picked = jnp.take_along_axis(line, lane[span], axis=1, mode="promise_in_bounds")
            found = picked if found is None else jnp.where(row[span] == r, picked, found)
        blocks.append(found)
    return jnp.concatenate(blocks, axis=0)


def pack_body(*refs):
    hbm, held = refs[:8], refs[13:21]
    out, first_x, last_x, first_theta, last_theta = refs[8:13]
    listed, slips, payload, staged, sems = refs[21:]
    copies = [
        pltpu.make_async_copy(source, target, sems.at[i])
        for i, (source, target) in enumerate(zip(hbm, held))
    ]
    for copy in copies:
        copy.start()
    for copy in copies[:7]:
        copy.wait()
    slip, size, growth, tile, lane, counts, order, block = held
    lines = listed.shape[0]
    peers = counts.shape[1]
    for j in range(lines):
        span = slice(j * LANES, (j + 1) * LANES)
        listed[j : j + 1, :] = order[0:1, span]
        for k in range(3):
            slips[k, j : j + 1, :] = slip[k : k + 1, span]
    s0, s1, s2 = slips[0], slips[1], slips[2]
    scale = size[...] * jnp.sqrt(1.0 + s0 * s0 + s1 * s1 + s2 * s2)
    payload[0] = scale * s0
    payload[1] = scale * s1
    payload[2] = scale * s2
    payload[3] = size[...] * growth[...]
    payload[4] = (tile[...] * LANES + lane[...]).astype(jnp.float32)
    count_rows = jnp.broadcast_to(counts[...], (peers, peers))
    below = lax.broadcasted_iota(jnp.int32, (peers, peers), 1) < lax.broadcasted_iota(
        jnp.int32, (peers, peers), 0
    )
    own = lax.broadcasted_iota(jnp.int32, (peers, peers), 1) == lax.broadcasted_iota(
        jnp.int32, (peers, peers), 0
    )
    start = jnp.sum(jnp.where(below, count_rows, 0), axis=1, keepdims=True)
    count = jnp.sum(jnp.where(own, count_rows, 0), axis=1, keepdims=True)
    shape = (peers, LANES)
    slot = lax.broadcasted_iota(jnp.int32, shape, 1)
    used = slot < count
    place = jnp.minimum(start + slot, lines * LANES - 1)
    bubble = take_rows(listed, place >> 7, place & 127)
    row, column = bubble >> 7, bubble & 127
    for k in range(4):
        value = take_rows(payload.at[k], row, column)
        staged[:, k, :] = jnp.where(used, value, 0.0)
    cell = take_rows(payload.at[4], row, column).astype(jnp.int32)
    cell = jnp.where(used, cell, 0)
    staged[:, 4, :] = (cell >> 8).astype(jnp.float32)
    staged[:, 5, :] = (cell & 255).astype(jnp.float32)
    staged[:, 6, :] = jnp.zeros(shape, jnp.float32)
    staged[:, 7, :] = jnp.zeros(shape, jnp.float32)
    out[...] = staged[...].astype(jnp.bfloat16)
    copies[7].wait()
    first_x[...] = block[:, :, 0, :].astype(jnp.bfloat16)
    last_x[...] = block[:, :, ROWS - 1, :].astype(jnp.bfloat16)
    first_theta[...] = block[:, 0].astype(jnp.bfloat16)
    last_theta[...] = block[:, block.shape[1] - 1].astype(jnp.bfloat16)


def radial_neighbours(v):
    column = lax.broadcasted_iota(jnp.int32, v.shape, 1)
    last = v.shape[1] - 1
    outer = jnp.where(column == last, 0.0, pltpu.roll(v, last, 1))
    inner = jnp.where(column == 0, 0.0, pltpu.roll(v, 1, 1))
    return outer, inner


def axial_neighbours(v, before, after):
    row = lax.broadcasted_iota(jnp.int32, v.shape, 0)
    ahead = jnp.where(row == ROWS - 1, after, pltpu.roll(v, ROWS - 1, 0))
    behind = jnp.where(row == 0, before, pltpu.roll(v, 1, 0))
    return ahead, behind


def after(arrays, event):
    count = len(arrays)
    return pl.pallas_call(
        lambda *refs: None,
        name="after",
        out_shape=tuple(jax.ShapeDtypeStruct(x.shape, x.dtype) for x in arrays),
        in_specs=[ANY] * (count + 1),
        out_specs=(ANY,) * count,
        input_output_aliases={i: i for i in range(count)},
        compiler_params=pltpu.CompilerParams(vmem_limit_bytes=60 * 1024 * 1024),
    )(*arrays, event)


def cell_hot(index_line, cells):
    row = lax.broadcasted_iota(jnp.int32, (cells, LANES), 0).astype(jnp.bfloat16)
    return row == jnp.broadcast_to(index_line, (cells, LANES))


def hot_rows(arrived, holders, cells):
    zero = jnp.zeros((cells, LANES), jnp.bfloat16)
    parts = [
        jnp.where(cell_hot(arrived[h][4:5, :], cells), jnp.ones_like(zero), zero) for h in holders
    ]
    return jnp.concatenate(parts, axis=1)


def hot_columns(arrived, holders, cells, component):
    zero = jnp.zeros((cells, LANES), jnp.bfloat16)
    parts = []
    for h in holders:
        value = jnp.broadcast_to(arrived[h][component : component + 1, :], zero.shape)
        parts.append(jnp.where(cell_hot(arrived[h][5:6, :], cells), value, zero))
    return jnp.concatenate(parts, axis=1)


def deposit(rows, columns):
    return lax.dot_general(
        rows, columns, (((1,), (1,)), ((), ())), preferred_element_type=jnp.float32
    )


def density_body(arrived, out):
    step = 4
    total = None
    for first in range(0, arrived.shape[0], step):
        holders = range(first, first + step)
        part = deposit(
            hot_rows(arrived, holders, out.shape[0]),
            hot_columns(arrived, holders, out.shape[1], 3),
        )
        total = part if total is None else total + part
    out[...] = total


def source_body(density, velocity, x_before, x_after, out, total, whole, staged, sems):
    th, width = velocity.shape[1], velocity.shape[3]
    radius = lax.broadcasted_iota(jnp.int32, (ROWS, width), 1).astype(jnp.float32)
    outward = (radius + 1.0) / (2.0 * radius + 1.0)
    inward = radius / (2.0 * radius + 1.0)
    for t in range(th):
        ahead, behind = axial_neighbours(velocity[0, t], 0.0, 0.0)
        around = ahead - behind
        if t < th - 1:
            around = around + velocity[1, t + 1]
        if t > 0:
            around = around - velocity[1, t - 1]
        outer, inner = radial_neighbours(velocity[2, t])
        span = slice(t * ROWS, (t + 1) * ROWS)
        total[span, :] = 0.5 * around + (outward * outer - inward * inner) + density[span, :]
    halves = whole.shape[0]
    blank = jnp.zeros((out.shape[1] - th - 2, LANES), jnp.float32)
    copies = []
    first = velocity[1, 0]
    last = velocity[1, th - 1]
    for half in range(halves):
        span = slice(half * LANES, (half + 1) * LANES)
        whole[half] = total[:, span]
        for x in range(ROWS):
            layer = whole[half, pl.ds(x, th, stride=ROWS), :]
            if x == 0:
                layer = layer - 0.5 * x_before[0, :, span].astype(jnp.float32)
            if x == ROWS - 1:
                layer = layer + 0.5 * x_after[0, :, span].astype(jnp.float32)
            ends = [first[x : x + 1, span], last[x : x + 1, span], blank]
            column = jnp.concatenate([layer] + ends, axis=0)
            staged[half * ROWS + x] = column.astype(jnp.bfloat16)
            if x % 4 == 3:
                four = pl.ds(half * ROWS + x - 3, 4)
                sem = sems.at[len(copies)]
                copies.append(pltpu.make_async_copy(staged.at[four], out.at[four], sem))
                copies[-1].start()
    for copy in copies:
        copy.wait()


def predictor_body(*refs):
    hbm, out, held = refs[:6], refs[6], refs[7:13]
    across, low, high, density, sems = refs[13:]
    arrived, velocity, theta_before, theta_after, x_before, x_after = held
    copies = [
        pltpu.make_async_copy(source, target, sems.at[i])
        for i, (source, target) in enumerate(zip(hbm, held))
    ]
    for copy in copies:
        copy.start()
    copies[0].wait()
    th, width = velocity.shape[1], velocity.shape[3]
    step = 4
    starts = range(0, arrived.shape[0], step)
    cells = density.shape[1]
    for start in starts:
        span = slice(start * LANES, (start + step) * LANES)
        across[:, span] = hot_rows(arrived, range(start, start + step), cells)
    for copy in copies[1:]:
        copy.wait()
    radius = lax.broadcasted_iota(jnp.int32, (ROWS, width), 1).astype(jnp.float32)
    outward = (radius + 1.0) / (radius + 0.5)
    inward = radius / (radius + 0.5)
    low[...] = x_before[...].astype(jnp.float32)
    high[...] = x_after[...].astype(jnp.float32)
    for c in range(3):
        total = None
        for start in starts:
            span = slice(start * LANES, (start + step) * LANES)
            columns = hot_columns(arrived, range(start, start + step), width, c)
            part = deposit(across[:, span], columns)
            total = part if total is None else total + part
        density[c] = total
        for t in range(th):
            v = velocity[c, t]
            ahead, behind = axial_neighbours(v, low[c, t : t + 1, :], high[c, t : t + 1, :])
            above = velocity[c, t + 1] if t < th - 1 else theta_after[c].astype(jnp.float32)
            under = velocity[c, t - 1] if t > 0 else theta_before[c].astype(jnp.float32)
            outer, inner = radial_neighbours(v)
            around = (ahead + behind) + (above + under) + (outward * outer + inward * inner)
            out[c, t] = (
                (1.0 - 6.0 * DIFFUSE) * v
                + DIFFUSE * around
                + density[c, t * ROWS : (t + 1) * ROWS, :]
            )


def in_parts(out, staged, sems, make):
    parts = sems.shape[0]
    rows = out.shape[0] // parts
    copies = []
    for i in range(parts):
        span = pl.ds(i * rows, rows)
        make(i * rows, rows)
        copies.append(pltpu.make_async_copy(staged.at[span], out.at[span], sems.at[i]))
        copies[-1].start()
    for copy in copies:
        copy.wait()


def transform_body(table, source, before, after, out, staged, sems):
    def make(first, rows):
        span = slice(first, first + rows)
        product = jnp.dot(table[span, :], source[...], preferred_element_type=jnp.float32)
        staged[span, :] = product.astype(jnp.bfloat16)

    in_parts(out, staged, sems, make)


def solve_body(spread, inverse, out, whole, staged, sems):
    rows = spread.shape[1]
    halves = whole.shape[0]
    for x in range(ROWS):
        for half in range(halves):
            layer = spread[half * ROWS + x].astype(jnp.float32)
            whole[half, pl.ds(x, rows, stride=ROWS), :] = layer
    group = 2 * ROWS

    def make(first, rows):
        for j in range(first // group, (first + rows) // group):
            span = slice(j * group, (j + 1) * group)
            pair = jnp.concatenate([whole[half, span, :] for half in range(halves)], axis=1)
            staged[span, :] = lax.dot_general(
                pair.astype(jnp.bfloat16),
                inverse[j],
                (((1,), (1,)), ((), ())),
                preferred_element_type=jnp.float32,
            )

    in_parts(out, staged, sems, make)


def spectral_table(length, blocks, extra):
    row = np.arange(length)[:, None]
    frequency = np.where(row == 1, length // 2, row // 2)
    angle = (frequency * np.arange(length)[None, :] % length) * (2.0 * math.pi / length)
    cosine = (row % 2 == 0) | (row == 1)
    table = np.where(cosine, np.cos(angle), np.sin(angle)) * math.sqrt(2.0 / length)
    step = length // blocks
    wide = np.zeros((length, blocks, step + extra))
    wide[:, :, :step] = table.reshape(length, blocks, step)
    starts = np.arange(blocks) * step
    wide[:, :, step] = 0.5 * table[:, (starts - 1) % length]
    wide[:, :, step + 1] = -0.5 * table[:, (starts + step) % length]
    return wide.reshape(length, -1).astype(jnp.bfloat16)


def ring(axis, step):
    count = lax.axis_size(axis)
    return [(i, (i + step) % count) for i in range(count)]


def on_device(
    velocity,
    bubble_slip,
    bubble_size,
    bubble_growth,
    bubble_tile,
    bubble_lane,
    send_counts,
    bubble_order,
    radial_inverse,
):
    _, th, ax, width = velocity.shape
    peers = send_counts.shape[1]
    bubbles = bubble_order.shape[1]
    lines = bubbles // LANES
    groups = lax.axis_size("az")
    f32, bf16 = jnp.float32, jnp.bfloat16
    struct = jax.ShapeDtypeStruct
    square = (lines, LANES)

    bubbles_in = (
        bubble_slip,
        bubble_size.reshape(square),
        bubble_growth.reshape(square),
        bubble_tile.reshape(square),
        bubble_lane.reshape(square),
        send_counts,
        bubble_order,
    )
    bubbles_in = bubbles_in + (velocity,)
    packed, first_x, last_x, first_theta, last_theta = call(
        pack_body,
        "pack_bubbles",
        (
            struct((peers, ROWS, LANES), bf16),
            struct((3, th, width), bf16),
            struct((3, th, width), bf16),
            struct((3, ax, width), bf16),
            struct((3, ax, width), bf16),
        ),
        bubbles_in,
        specs=[ANY] * 8,
        limit=60,
        scratch=tuple(pltpu.VMEM(x.shape, x.dtype) for x in bubbles_in)
        + (
            pltpu.VMEM(square, jnp.int32),
            pltpu.VMEM((3,) + square, f32),
            pltpu.VMEM((5,) + square, f32),
            pltpu.VMEM((peers, ROWS, LANES), f32),
            pltpu.SemaphoreType.DMA((8,)),
        ),
    )
    arrived = lax.all_to_all(packed, "ax", split_axis=0, concat_axis=0, tiled=True)

    x_before = lax.ppermute(last_x, "ax", ring("ax", 1))
    x_after = lax.ppermute(first_x, "ax", ring("ax", -1))
    slots = peers * LANES
    cells = th * ax
    extra = 8
    halves = width // LANES
    density = call(
        density_body,
        "density",
        struct((cells, width), f32),
        (arrived,),
        flops=2 * cells * slots * width,
    )
    source = call(
        source_body,
        "source",
        struct((groups, th + extra, LANES), bf16),
        (density, velocity, x_before, x_after),
        out_specs=ANY,
        scratch=(
            pltpu.VMEM((cells, width), f32),
            pltpu.VMEM((halves, cells, LANES), f32),
            pltpu.VMEM((groups, th + extra, LANES), bf16),
            pltpu.SemaphoreType.DMA((groups // 4,)),
        ),
        flops=30 * cells * width,
    )
    gathered = lax.all_to_all(source, "az", split_axis=0, concat_axis=0, tiled=True)

    first_layer, last_layer = after((first_theta, last_theta), source)
    theta_before = lax.ppermute(last_layer, "az", ring("az", 1))
    theta_after = lax.ppermute(first_layer, "az", ring("az", -1))

    beside = (arrived, velocity, theta_before, theta_after, x_before, x_after)
    predicted = call(
        predictor_body,
        "predictor",
        struct(velocity.shape, f32),
        beside,
        specs=[ANY] * 6,
        scratch=tuple(pltpu.VMEM(x.shape, x.dtype) for x in beside)
        + (
            pltpu.VMEM((cells, slots), bf16),
            pltpu.VMEM((3, th, width), f32),
            pltpu.VMEM((3, th, width), f32),
            pltpu.VMEM((3, cells, width), f32),
            pltpu.SemaphoreType.DMA((6,)),
        ),
        flops=2 * 3 * cells * slots * width,
        limit=56,
    )

    length = groups * th
    table = jnp.asarray(spectral_table(length, groups, extra))
    coefficients = call(
        transform_body,
        "transform",
        struct((length, LANES), bf16),
        (table, gathered.reshape(-1, LANES), theta_before, theta_after),
        specs=[VMEM, VMEM, ANY, ANY],
        out_specs=ANY,
        scratch=(pltpu.VMEM((length, LANES), bf16), pltpu.SemaphoreType.DMA((2,))),
        flops=2 * length * (length + groups * extra) * LANES,
    )
    spread = lax.all_to_all(
        coefficients.reshape(groups, th, LANES), "az", split_axis=0, concat_axis=0, tiled=True
    )
    modes = call(
        solve_body,
        "solve",
        struct((th * ax, width), f32),
        (spread, radial_inverse),
        out_specs=ANY,
        scratch=(
            pltpu.VMEM((halves, cells, LANES), f32),
            pltpu.VMEM((cells, width), f32),
            pltpu.SemaphoreType.DMA((4,)),
        ),
        flops=2 * th * ax * width * width,
    )
    return predicted, modes.reshape(th, ax, width)


def solution(mesh):
    placed = (
        P(None, "az", "ax", None),
        P(None, ("az", "ax")),
        P(("az", "ax")),
        P(("az", "ax")),
        P(("az", "ax")),
        P(("az", "ax")),
        P(("az", "ax"), None),
        P(("az", "ax"), None),
        P("az", None, None),
    )
    return jax.shard_map(
        on_device,
        mesh=mesh,
        in_specs=placed,
        out_specs=(P(None, "az", "ax", None), P("az", "ax", None)),
        check_vma=False,
    )
```

```python
import functools
import math

import jax
import jax.numpy as jnp
import numpy as np
from jax import lax
from jax.experimental import pallas as pl
from jax.experimental.pallas import tpu as pltpu
from jax.sharding import PartitionSpec as P

DIFFUSE = 0.12
LANES = 128
ROWS = 8

VMEM = pl.BlockSpec(memory_space=pltpu.VMEM)
ANY = pl.BlockSpec(memory_space=pl.ANY)


def call(
    body, name, out_shape, operands, scratch=(), specs=None, flops=0, limit=24, out_specs=None,
    aliases=None,
):
    moved = sum(x.size * x.dtype.itemsize for x in operands)
    return pl.pallas_call(
        body,
        name=name,
        out_shape=out_shape,
        in_specs=[VMEM] * len(operands) if specs is None else specs,
        out_specs=jax.tree.map(lambda _: VMEM, out_shape) if out_specs is None else out_specs,
        input_output_aliases=aliases or {},
        scratch_shapes=list(scratch),
        compiler_params=pltpu.CompilerParams(vmem_limit_bytes=limit * 1024 * 1024),
        cost_estimate=pl.CostEstimate(flops=flops, bytes_accessed=moved, transcendentals=0),
    )(*operands)


def take_rows(table, row, lane):
    blocks = []
    for first in range(0, row.shape[0], ROWS):
        span = slice(first, first + ROWS)
        found = None
        for r in range(table.shape[0]):
            line = jnp.broadcast_to(table[r : r + 1, :], (ROWS, LANES))
            picked = jnp.take_along_axis(line, lane[span], axis=1, mode="promise_in_bounds")
            found = picked if found is None else jnp.where(row[span] == r, picked, found)
        blocks.append(found)
    return jnp.concatenate(blocks, axis=0)


def pack_body(*refs):
    hbm, held = refs[:8], refs[13:21]
    results = refs[8:13]
    listed, slips, payload, staged, sems = refs[21:26]
    packed, *layers = made = refs[26:31]
    sent = refs[31]
    copies = [
        pltpu.make_async_copy(source, target, sems.at[i])
        for i, (source, target) in enumerate(zip(hbm, held))
    ]
    for copy in copies:
        copy.start()
    for copy in copies[:7]:
        copy.wait()
    slip, size, growth, tile, lane, counts, order, block = held
    lines = listed.shape[0]
    peers = counts.shape[1]
    for j in range(lines):
        span = slice(j * LANES, (j + 1) * LANES)
        listed[j : j + 1, :] = order[0:1, span]
        for k in range(3):
            slips[k, j : j + 1, :] = slip[k : k + 1, span]
    s0, s1, s2 = slips[0], slips[1], slips[2]
    scale = size[...] * jnp.sqrt(1.0 + s0 * s0 + s1 * s1 + s2 * s2)
    payload[0] = scale * s0
    payload[1] = scale * s1
    payload[2] = scale * s2
    payload[3] = size[...] * growth[...]
    payload[4] = (tile[...] * LANES + lane[...]).astype(jnp.float32)
    count_rows = jnp.broadcast_to(counts[...], (peers, peers))
    below = lax.broadcasted_iota(jnp.int32, (peers, peers), 1) < lax.broadcasted_iota(
        jnp.int32, (peers, peers), 0
    )
    own = lax.broadcasted_iota(jnp.int32, (peers, peers), 1) == lax.broadcasted_iota(
        jnp.int32, (peers, peers), 0
    )
    start = jnp.sum(jnp.where(below, count_rows, 0), axis=1, keepdims=True)
    count = jnp.sum(jnp.where(own, count_rows, 0), axis=1, keepdims=True)
    shape = (peers, LANES)
    slot = lax.broadcasted_iota(jnp.int32, shape, 1)
    used = slot < count
    place = jnp.minimum(start + slot, lines * LANES - 1)
    bubble = take_rows(listed, place >> 7, place & 127)
    copies[7].wait()
    layers[0][...] = block[:, :, 0, :].astype(jnp.bfloat16)
    layers[1][...] = block[:, :, ROWS - 1, :].astype(jnp.bfloat16)
    layers[2][...] = block[:, 0].astype(jnp.bfloat16)
    layers[3][...] = block[:, block.shape[1] - 1].astype(jnp.bfloat16)
    leaving = [
        pltpu.make_async_copy(made[i], results[i], sent.at[i - 1]) for i in range(1, len(made))
    ]
    for copy in leaving:
        copy.start()
    blank = jnp.zeros((ROWS, LANES), jnp.float32)
    for first in range(0, peers, ROWS):
        span = slice(first, first + ROWS)
        row, column = bubble[span] >> 7, bubble[span] & 127
        for k in range(4):
            value = take_rows(payload.at[k], row, column)
            staged[span, k, :] = jnp.where(used[span], value, 0.0)
        cell = take_rows(payload.at[4], row, column).astype(jnp.int32)
        cell = jnp.where(used[span], cell, 0)
        staged[span, 4, :] = (cell >> 8).astype(jnp.float32)
        staged[span, 5, :] = (cell & 255).astype(jnp.float32)
        staged[span, 6, :] = blank
        staged[span, 7, :] = blank
        packed[span] = staged[span].astype(jnp.bfloat16)
        eight = pl.ds(first, ROWS)
        copy = pltpu.make_async_copy(
            packed.at[eight], results[0].at[eight], sent.at[len(leaving)]
        )
        copy.start()
        leaving.append(copy)
    for copy in leaving:
        copy.wait()


def radial_neighbours(v):
    column = lax.broadcasted_iota(jnp.int32, v.shape, 1)
    last = v.shape[1] - 1
    outer = jnp.where(column == last, 0.0, pltpu.roll(v, last, 1))
    inner = jnp.where(column == 0, 0.0, pltpu.roll(v, 1, 1))
    return outer, inner


def axial_neighbours(v, before, after):
    row = lax.broadcasted_iota(jnp.int32, v.shape, 0)
    ahead = jnp.where(row == ROWS - 1, after, pltpu.roll(v, ROWS - 1, 0))
    behind = jnp.where(row == 0, before, pltpu.roll(v, 1, 0))
    return ahead, behind


def after(arrays, event):
    count = len(arrays)
    return pl.pallas_call(
        lambda *refs: None,
        name="after",
        out_shape=tuple(jax.ShapeDtypeStruct(x.shape, x.dtype) for x in arrays),
        in_specs=[ANY] * (count + 1),
        out_specs=(ANY,) * count,
        input_output_aliases={i: i for i in range(count)},
        compiler_params=pltpu.CompilerParams(vmem_limit_bytes=60 * 1024 * 1024),
    )(*arrays, event)


def cell_hot(index_line, cells):
    row = lax.broadcasted_iota(jnp.int32, (cells, LANES), 0).astype(jnp.bfloat16)
    return row == jnp.broadcast_to(index_line, (cells, LANES))


def hot_rows(arrived, holders, cells):
    zero = jnp.zeros((cells, LANES), jnp.bfloat16)
    parts = [
        jnp.where(cell_hot(arrived[h][4:5, :], cells), jnp.ones_like(zero), zero) for h in holders
    ]
    return jnp.concatenate(parts, axis=1)


def hot_columns(arrived, holders, cells, component):
    zero = jnp.zeros((cells, LANES), jnp.bfloat16)
    parts = []
    for h in holders:
        value = jnp.broadcast_to(arrived[h][component : component + 1, :], zero.shape)
        parts.append(jnp.where(cell_hot(arrived[h][5:6, :], cells), value, zero))
    return jnp.concatenate(parts, axis=1)


def deposit(rows, columns):
    return lax.dot_general(
        rows, columns, (((1,), (1,)), ((), ())), preferred_element_type=jnp.float32
    )


def density_body(arrived, out):
    step = 4
    total = None
    for first in range(0, arrived.shape[0], step):
        holders = range(first, first + step)
        part = deposit(
            hot_rows(arrived, holders, out.shape[0]),
            hot_columns(arrived, holders, out.shape[1], 3),
        )
        total = part if total is None else total + part
    out[...] = total


def source_body(density, velocity, x_before, x_after, out, total, whole, staged, sems):
    th, width = velocity.shape[1], velocity.shape[3]
    radius = lax.broadcasted_iota(jnp.int32, (ROWS, width), 1).astype(jnp.float32)
    outward = (radius + 1.0) / (2.0 * radius + 1.0)
    inward = radius / (2.0 * radius + 1.0)
    for t in range(th):
        ahead, behind = axial_neighbours(velocity[0, t], 0.0, 0.0)
        around = ahead - behind
        if t < th - 1:
            around = around + velocity[1, t + 1]
        if t > 0:
            around = around - velocity[1, t - 1]
        outer, inner = radial_neighbours(velocity[2, t])
        span = slice(t * ROWS, (t + 1) * ROWS)
        total[span, :] = 0.5 * around + (outward * outer - inward * inner) + density[span, :]
    halves = whole.shape[0]
    blank = jnp.zeros((out.shape[1] - th - 2, LANES), jnp.float32)
    copies = []
    first = velocity[1, 0]
    last = velocity[1, th - 1]
    for half in range(halves):
        span = slice(half * LANES, (half + 1) * LANES)
        whole[half] = total[:, span]
        for x in range(ROWS):
            layer = whole[half, pl.ds(x, th, stride=ROWS), :]
            if x == 0:
                layer = layer - 0.5 * x_before[0, :, span].astype(jnp.float32)
            if x == ROWS - 1:
                layer = layer + 0.5 * x_after[0, :, span].astype(jnp.float32)
            ends = [first[x : x + 1, span], last[x : x + 1, span], blank]
            column = jnp.concatenate([layer] + ends, axis=0)
            staged[half * ROWS + x] = column.astype(jnp.bfloat16)
            if x % 4 == 3:
                four = pl.ds(half * ROWS + x - 3, 4)
                sem = sems.at[len(copies)]
                copies.append(pltpu.make_async_copy(staged.at[four], out.at[four], sem))
                copies[-1].start()
    for copy in copies:
        copy.wait()


def predictor_body(*refs):
    hbm, out, held = refs[:6], refs[6], refs[7:13]
    across, low, high, density, sems = refs[13:]
    arrived, velocity, theta_before, theta_after, x_before, x_after = held
    copies = [
        pltpu.make_async_copy(source, target, sems.at[i])
        for i, (source, target) in enumerate(zip(hbm, held))
    ]
    for copy in copies:
        copy.start()
    copies[0].wait()
    th, width = velocity.shape[1], velocity.shape[3]
    step = 4
    starts = range(0, arrived.shape[0], step)
    cells = density.shape[1]
    for start in starts:
        span = slice(start * LANES, (start + step) * LANES)
        across[:, span] = hot_rows(arrived, range(start, start + step), cells)
    for copy in copies[1:]:
        copy.wait()
    radius = lax.broadcasted_iota(jnp.int32, (ROWS, width), 1).astype(jnp.float32)
    outward = (radius + 1.0) / (radius + 0.5)
    inward = radius / (radius + 0.5)
    low[...] = x_before[...].astype(jnp.float32)
    high[...] = x_after[...].astype(jnp.float32)
    for c in range(3):
        total = None
        for start in starts:
            span = slice(start * LANES, (start + step) * LANES)
            columns = hot_columns(arrived, range(start, start + step), width, c)
            part = deposit(across[:, span], columns)
            total = part if total is None else total + part
        density[c] = total
        for t in range(th):
            v = velocity[c, t]
            ahead, behind = axial_neighbours(v, low[c, t : t + 1, :], high[c, t : t + 1, :])
            above = velocity[c, t + 1] if t < th - 1 else theta_after[c].astype(jnp.float32)
            under = velocity[c, t - 1] if t > 0 else theta_before[c].astype(jnp.float32)
            outer, inner = radial_neighbours(v)
            around = (ahead + behind) + (above + under) + (outward * outer + inward * inner)
            out[c, t] = (
                (1.0 - 6.0 * DIFFUSE) * v
                + DIFFUSE * around
                + density[c, t * ROWS : (t + 1) * ROWS, :]
            )


def in_parts(out, staged, sems, make):
    parts = sems.shape[0]
    rows = out.shape[0] // parts
    copies = []
    for i in range(parts):
        span = pl.ds(i * rows, rows)
        make(i * rows, rows)
        copies.append(pltpu.make_async_copy(staged.at[span], out.at[span], sems.at[i]))
        copies[-1].start()
    for copy in copies:
        copy.wait()


def transform_body(table, source, before, after, out, staged, sems):
    def make(first, rows):
        span = slice(first, first + rows)
        product = jnp.dot(table[span, :], source[...], preferred_element_type=jnp.float32)
        staged[span, :] = product.astype(jnp.bfloat16)

    in_parts(out, staged, sems, make)


def solve_body(spread, inverse, out, whole, staged, sems):
    rows = spread.shape[1]
    halves = whole.shape[0]
    for x in range(ROWS):
        for half in range(halves):
            layer = spread[half * ROWS + x].astype(jnp.float32)
            whole[half, pl.ds(x, rows, stride=ROWS), :] = layer
    group = 2 * ROWS

    def make(first, rows):
        for j in range(first // group, (first + rows) // group):
            span = slice(j * group, (j + 1) * group)
            pair = jnp.concatenate([whole[half, span, :] for half in range(halves)], axis=1)
            staged[span, :] = lax.dot_general(
                pair.astype(jnp.bfloat16),
                inverse[j],
                (((1,), (1,)), ((), ())),
                preferred_element_type=jnp.float32,
            )

    in_parts(out, staged, sems, make)


def spectral_table(length, blocks, extra):
    row = np.arange(length)[:, None]
    frequency = np.where(row == 1, length // 2, row // 2)
    angle = (frequency * np.arange(length)[None, :] % length) * (2.0 * math.pi / length)
    cosine = (row % 2 == 0) | (row == 1)
    table = np.where(cosine, np.cos(angle), np.sin(angle)) * math.sqrt(2.0 / length)
    step = length // blocks
    wide = np.zeros((length, blocks, step + extra))
    wide[:, :, :step] = table.reshape(length, blocks, step)
    starts = np.arange(blocks) * step
    wide[:, :, step] = 0.5 * table[:, (starts - 1) % length]
    wide[:, :, step + 1] = -0.5 * table[:, (starts + step) % length]
    return wide.reshape(length, -1).astype(jnp.bfloat16)


def ring(axis, step):
    count = lax.axis_size(axis)
    return [(i, (i + step) % count) for i in range(count)]


def on_device(
    velocity,
    bubble_slip,
    bubble_size,
    bubble_growth,
    bubble_tile,
    bubble_lane,
    send_counts,
    bubble_order,
    radial_inverse,
):
    _, th, ax, width = velocity.shape
    peers = send_counts.shape[1]
    bubbles = bubble_order.shape[1]
    lines = bubbles // LANES
    groups = lax.axis_size("az")
    f32, bf16 = jnp.float32, jnp.bfloat16
    struct = jax.ShapeDtypeStruct
    square = (lines, LANES)

    bubbles_in = (
        bubble_slip,
        bubble_size.reshape(square),
        bubble_growth.reshape(square),
        bubble_tile.reshape(square),
        bubble_lane.reshape(square),
        send_counts,
        bubble_order,
    )
    bubbles_in = bubbles_in + (velocity,)
    packed, first_x, last_x, first_theta, last_theta = call(
        pack_body,
        "pack_bubbles",
        (
            struct((peers, ROWS, LANES), bf16),
            struct((3, th, width), bf16),
            struct((3, th, width), bf16),
            struct((3, ax, width), bf16),
            struct((3, ax, width), bf16),
        ),
        bubbles_in,
        specs=[ANY] * 8,
        out_specs=(ANY,) * 5,
        limit=60,
        scratch=tuple(pltpu.VMEM(x.shape, x.dtype) for x in bubbles_in)
        + (
            pltpu.VMEM(square, jnp.int32),
            pltpu.VMEM((3,) + square, f32),
            pltpu.VMEM((5,) + square, f32),
            pltpu.VMEM((peers, ROWS, LANES), f32),
            pltpu.SemaphoreType.DMA((8,)),
            pltpu.VMEM((peers, ROWS, LANES), bf16),
            pltpu.VMEM((3, th, width), bf16),
            pltpu.VMEM((3, th, width), bf16),
            pltpu.VMEM((3, ax, width), bf16),
            pltpu.VMEM((3, ax, width), bf16),
            pltpu.SemaphoreType.DMA((4 + peers // ROWS,)),
        ),
    )
    arrived = lax.all_to_all(packed, "ax", split_axis=0, concat_axis=0, tiled=True)

    x_before = lax.ppermute(last_x, "ax", ring("ax", 1))
    x_after = lax.ppermute(first_x, "ax", ring("ax", -1))
    slots = peers * LANES
    cells = th * ax
    extra = 8
    halves = width // LANES
    density = call(
        density_body,
        "density",
        struct((cells, width), f32),
        (arrived,),
        flops=2 * cells * slots * width,
    )
    source = call(
        source_body,
        "source",
        struct((groups, th + extra, LANES), bf16),
        (density, velocity, x_before, x_after),
        out_specs=ANY,
        scratch=(
            pltpu.VMEM((cells, width), f32),
            pltpu.VMEM((halves, cells, LANES), f32),
            pltpu.VMEM((groups, th + extra, LANES), bf16),
            pltpu.SemaphoreType.DMA((groups // 4,)),
        ),
        flops=30 * cells * width,
    )
    gathered = lax.all_to_all(source, "az", split_axis=0, concat_axis=0, tiled=True)

    first_layer, last_layer = after((first_theta, last_theta), source)
    theta_before = lax.ppermute(last_layer, "az", ring("az", 1))
    theta_after = lax.ppermute(first_layer, "az", ring("az", -1))

    beside = (arrived, velocity, theta_before, theta_after, x_before, x_after)
    predicted = call(
        predictor_body,
        "predictor",
        struct(velocity.shape, f32),
        beside,
        specs=[ANY] * 6,
        scratch=tuple(pltpu.VMEM(x.shape, x.dtype) for x in beside)
        + (
            pltpu.VMEM((cells, slots), bf16),
            pltpu.VMEM((3, th, width), f32),
            pltpu.VMEM((3, th, width), f32),
            pltpu.VMEM((3, cells, width), f32),
            pltpu.SemaphoreType.DMA((6,)),
        ),
        flops=2 * 3 * cells * slots * width,
        limit=56,
    )

    length = groups * th
    table = jnp.asarray(spectral_table(length, groups, extra))
    coefficients = call(
        transform_body,
        "transform",
        struct((length, LANES), bf16),
        (table, gathered.reshape(-1, LANES), theta_before, theta_after),
        specs=[VMEM, VMEM, ANY, ANY],
        out_specs=ANY,
        scratch=(pltpu.VMEM((length, LANES), bf16), pltpu.SemaphoreType.DMA((2,))),
        flops=2 * length * (length + groups * extra) * LANES,
    )
    spread = lax.all_to_all(
        coefficients.reshape(groups, th, LANES), "az", split_axis=0, concat_axis=0, tiled=True
    )
    modes = call(
        solve_body,
        "solve",
        struct((th * ax, width), f32),
        (spread, radial_inverse),
        out_specs=ANY,
        scratch=(
            pltpu.VMEM((halves, cells, LANES), f32),
            pltpu.VMEM((cells, width), f32),
            pltpu.SemaphoreType.DMA((4,)),
        ),
        flops=2 * th * ax * width * width,
    )
    return predicted, modes.reshape(th, ax, width)


def solution(mesh):
    placed = (
        P(None, "az", "ax", None),
        P(None, ("az", "ax")),
        P(("az", "ax")),
        P(("az", "ax")),
        P(("az", "ax")),
        P(("az", "ax")),
        P(("az", "ax"), None),
        P(("az", "ax"), None),
        P("az", None, None),
    )
    return jax.shard_map(
        on_device,
        mesh=mesh,
        in_specs=placed,
        out_specs=(P(None, "az", "ax", None), P("az", "ax", None)),
        check_vma=False,
    )
```
